32 devices in a mesh: orb: 4 (over x, core), box: 8 (over z, y).
Axes of the slice: x: 2, y: 2, z: 4, core: 2. Of those that a mesh axis runs over, the one named last changes fastest.
Arguments:
- orbitals: bfloat16 [32, 48, 2304], P(('orb', 'box')), may hold values from -6 to 6
- corners: int32 [32, 3], replicated, may hold values from 0 to 8
- pairs: int32 [384, 2], P(('orb', 'box')), may hold values from 0 to 11, as said below
- counts: int32 [32], P(('orb', 'box')), may hold values from 1 to 12, as said below
Outputs:
- exchange: bfloat16 [32, 48, 2304], P(('orb', 'box'))
- gram: float32 [8, 4, 4], P('box')
The draws below stay inside these ranges and needn't reach their ends.
Inputs may be any that keep to these rules, and one draw needn't show every extreme that they name: pairs[s, 0] is below 4 and pairs[s, 1] below 12; slots at or beyond their device's count are not used. `counts`: some device has all 12 slots live.
All inputs are finite; a program needn't handle non-finite values.
Results may differ from the reference program's by a relative error of at most 0.0049.
Values may be sent and summed in bfloat16 or wider, within the bound.
A program may use at most 192 MiB of HBM per device.

```python
import math
import jax
import jax.numpy as jnp
from jax import lax

BOX = 48
SPAN = 8
ORB_DEV = 1
PAIR_DEV = 12
REGION_ORBITALS = 4
NORB = 32
PAIR_SLOT_TOTAL = 384
N_BOX = 8
DEVICES = 32


def draw_pairs(key, part):
    key = jax.random.fold_in(key, 11)
    leading_column = jax.random.randint(jax.random.fold_in(key, 1), (PAIR_SLOT_TOTAL, 1), 0, REGION_ORBITALS)
    partner_column = jax.random.randint(jax.random.fold_in(key, 2), (PAIR_SLOT_TOTAL, 1), 0, 3 * REGION_ORBITALS)
    return jnp.concatenate([leading_column, partner_column], axis=1).astype(jnp.int32)


def draw_counts(key, part):
    key = jax.random.fold_in(key, 23)
    base_counts = jax.random.randint(jax.random.fold_in(key, 1), (DEVICES,), 1, PAIR_DEV + 1)
    busiest = jax.random.randint(jax.random.fold_in(key, 2), (), 0, DEVICES)
    device_ids = jnp.arange(DEVICES, dtype=jnp.int32)
    return jnp.where(device_ids == busiest, PAIR_DEV, base_counts).astype(jnp.int32)


def with_ends(values, key, least, top_value):
    shape = values.shape
    spot = [jax.random.randint(jax.random.fold_in(key, axis), (), 0, shape[axis]) for axis in range(len(shape))]
    values = values.at[tuple(spot)].set(least)
    longest = shape.index(max(shape))
    spot[longest] = (spot[longest] + 1) % shape[longest]
    return values.at[tuple(spot)].set(top_value)


def block_levels(own_key, shape, split, least, largest):
    loudness, own = 1.0, jax.random.fold_in(own_key, 6)
    for dim, blocks in split:
        heights = jnp.exp(jax.random.uniform(jax.random.fold_in(own, dim), (blocks,), jnp.float32, least / len(split), largest / len(split)))
        loudness = loudness * jnp.repeat(heights, shape[dim] // blocks).reshape([-1 if axis == dim else 1 for axis in range(len(shape))])
    return loudness


def scatter_about(key, dims, scale, most, split=(), kind=jnp.bfloat16):
    values = scale * jax.random.normal(key, dims, jnp.float32)
    if split:
        values = values * block_levels(key, dims, split, -0.22, 0.18)
    return jnp.clip(values, -most, most).astype(kind)


def setup_inputs(seed: int = 0) -> dict:
    arg_keys = jax.random.split(jax.random.key(seed), 5)
    orbitals = scatter_about(arg_keys[0], (NORB, BOX, BOX * BOX), 1.0, 6.0, ((0, 32),))
    corners = with_ends(jax.random.randint(arg_keys[1], (NORB, 3), 0, SPAN + 1), jax.random.fold_in(arg_keys[1], 1), 0, SPAN).astype(jnp.int32)
    pairs = draw_pairs(jax.random.fold_in(arg_keys[4], 71), 0)
    counts = draw_counts(jax.random.fold_in(arg_keys[4], 71), 0)
    return {"orbitals": orbitals, "corners": corners, "pairs": pairs, "counts": counts}


screen_term = 0.5


def green_table(box_side):
    cell_index = jnp.arange(box_side, dtype=jnp.int32)
    wave = jnp.minimum(cell_index, box_side - cell_index).astype(jnp.float32) * (2.0 * math.pi / box_side)
    squared_modulus = wave * wave
    total = squared_modulus[:, None, None] + squared_modulus[None, :, None] + squared_modulus[None, None, :]
    return 1.0 / (total + screen_term)


def coulomb(density):
    green_kernel = green_table(BOX)
    return jnp.real(jnp.fft.ifftn(green_kernel * jnp.fft.fftn(density))).astype(jnp.float32)


def place(grid_values, anchor):
    padded = jnp.pad(grid_values, SPAN)
    return lax.dynamic_slice(padded, (anchor[0], anchor[1], anchor[2]), (BOX, BOX, BOX))


def global_id(region_id, window_pos):
    section_of = window_pos // REGION_ORBITALS
    member_of = window_pos % REGION_ORBITALS
    neighbour = (region_id + section_of - 1 + N_BOX) % N_BOX
    return (((member_of // ORB_DEV) * N_BOX + neighbour) * ORB_DEV + member_of % ORB_DEV).astype(jnp.int32)


def reference(orbitals, corners, pairs, counts):
    cubes = orbitals.reshape(NORB, BOX, BOX, BOX)
    slot_numbers = jnp.arange(PAIR_SLOT_TOTAL, dtype=jnp.int32)
    device_of = slot_numbers // PAIR_DEV
    region_of = device_of % N_BOX
    live_mask = (slot_numbers % PAIR_DEV < counts[device_of]).astype(jnp.float32)
    first_ids = global_id(region_of, REGION_ORBITALS + pairs[:, 0])
    second_ids = global_id(region_of, pairs[:, 1])

    def one_pair(totals, pair_item):
        first_id, second_id, pair_weight = pair_item
        phi_first = cubes[first_id].astype(jnp.float32)
        phi_second = cubes[second_id].astype(jnp.float32)
        offset = corners[second_id] - corners[first_id]
        second_here = place(phi_second, SPAN - offset)
        potential = coulomb(phi_first * second_here)
        totals = totals.at[first_id].add(-pair_weight * potential * second_here)
        totals = totals.at[second_id].add(-pair_weight * place(potential * phi_first, SPAN + offset))
        return totals, None

    totals, _ = lax.scan(one_pair, jnp.zeros((NORB, BOX, BOX, BOX), jnp.float32),
                         (first_ids, second_ids, live_mask))

    def gram_entry(position):
        region_id = position // (REGION_ORBITALS * REGION_ORBITALS)
        row_orb = global_id(region_id, REGION_ORBITALS + (position // REGION_ORBITALS) % REGION_ORBITALS)
        col_orb = global_id(region_id, REGION_ORBITALS + position % REGION_ORBITALS)
        offset = corners[row_orb] - corners[col_orb]
        moved = place(cubes[row_orb].astype(jnp.float32), SPAN - offset)
        return jnp.sum(moved * totals[col_orb]) / (BOX ** 3)

    gram = lax.map(gram_entry, jnp.arange(N_BOX * REGION_ORBITALS * REGION_ORBITALS, dtype=jnp.int32))
    exchange = totals.reshape(NORB, BOX, BOX * BOX).astype(jnp.bfloat16)
    return exchange, gram.reshape(N_BOX, REGION_ORBITALS, REGION_ORBITALS)
```

```python
import functools
import math

import jax
import jax.numpy as jnp
import ml_dtypes
import numpy as np
from jax import lax
from jax.experimental import pallas as pl
from jax.experimental.pallas import tpu as pltpu
from jax.sharding import PartitionSpec as P

SPAN = 8
SCREEN = 0.5
HALF = 64
LANES = 128
STEP = 8
F32 = jnp.float32
BF16 = jnp.bfloat16


def tables(box):
    n = np.arange(box)
    angle = (n[:, None] * n[None, :] % box) * (2.0 * math.pi / box)
    cas = np.cos(angle) + np.sin(angle)
    hi = cas.astype(ml_dtypes.bfloat16)
    lo = (cas - hi.astype(np.float64)).astype(ml_dtypes.bfloat16)
    rows = np.concatenate([hi, hi, lo], axis=1)
    lanes = np.zeros((2 * LANES, 2 * LANES), ml_dtypes.bfloat16)
    for p in range(2):
        s = slice(HALF * p, HALF * p + box)
        t = slice(LANES + HALF * p, LANES + HALF * p + box)
        lanes[s, s] = hi
        lanes[t, s] = hi
        lanes[s, t] = lo
    k = np.minimum(n, box - n) * (2.0 * math.pi / box)
    k2 = k * k
    g = -1.0 / (k2[:, None, None] + k2[None, :, None] + k2[None, None, :] + SCREEN) / box**3
    green = np.zeros((box, box, LANES), np.float32)
    for p in range(2):
        green[:, :, HALF * p : HALF * p + box] = g
    return rows, lanes, green


def lane_ids(rows):
    return lax.broadcasted_iota(jnp.int32, (rows, LANES), 1)


def unpack_step(box, blocks, lane):
    out = []
    for t in range(STEP):
        start = box * t
        blk, off = start // LANES, start % LANES
        x = blocks[blk]
        if off + box > LANES:
            x = jnp.where(lane >= off, x, blocks[blk + 1])
        out.append((x, off))
    return out


def unpack_pair(box, first, second, lane):
    out = []
    for (x, off), (y, _) in zip(unpack_step(box, first, lane), unpack_step(box, second, lane)):
        a = pltpu.roll(x, (-off) % LANES, 1) if off else x
        b = pltpu.roll(y, (HALF - off) % LANES, 1) if off != HALF else y
        both = jnp.where(lane < HALF, a, b)
        out.append(jnp.where(lane % HALF < box, both, 0.0))
    return out


def pack_blocks(box, rows, shift, lane):
    n_blocks = box * STEP // LANES
    blocks = [None] * n_blocks
    for t in range(STEP):
        start = box * t
        amount = (start - shift) % LANES
        x = pltpu.roll(rows[t], amount, 1) if amount else rows[t]
        for blk in range(start // LANES, (start + box - 1) // LANES + 1):
            lo = start - blk * LANES
            if blocks[blk] is None:
                blocks[blk] = x
            else:
                blocks[blk] = jnp.where(lane >= max(lo, 0), x, blocks[blk])
    return blocks


def load_blocks(box, ref, lead, g):
    width = box * STEP
    start = pl.multiple_of(g * width, LANES)
    return [
        ref[(*lead, slice(None), pl.ds(start + LANES * k, LANES))].astype(F32)
        for k in range(width // LANES)
    ]


def split_rows(x):
    hi = x.astype(BF16)
    lo = (x - hi.astype(F32)).astype(BF16)
    return hi, lo


def row_transform(t_rows, xs):
    x = jnp.concatenate(xs, axis=1)
    hi, lo = split_rows(x)
    stacked = jnp.concatenate([hi, lo, hi], axis=0)
    y = jnp.dot(t_rows, stacked, preferred_element_type=F32)
    return y[:, :LANES], y[:, LANES:]


def lane_transform(t_lanes, x):
    hi, lo = split_rows(x)
    y = jnp.dot(jnp.concatenate([hi, lo], axis=1), t_lanes, preferred_element_type=F32)
    return y[:, :LANES] + y[:, LANES:]


def pair_kernel(
    dims, corners, pairs, counts, cubes, rows_ref, lanes_ref, green, out, held, acc, work, u_all, phi_all
):
    box, own, blocks, regions = dims
    region_size = own * blocks
    n_cubes = 3 * region_size
    box_index = lax.axis_index("box")
    lane = lane_ids(box)
    steps = box // STEP
    zero8 = jnp.zeros((SPAN, LANES), F32)

    def place_of(member, section):
        return (member // own) * (3 * own) + section * own + member % own

    def id_of(member, section):
        neighbour = lax.rem(box_index + section - 1 + regions, regions)
        return ((member // own) * regions + neighbour) * own + member % own

    def unpack(item, _):
        q, g = item // steps, item % steps
        first = load_blocks(box, cubes, (2 * q,), g)
        second = load_blocks(box, cubes, (2 * q + 1,), g)
        for t, row in enumerate(unpack_pair(box, first, second, lane)):
            b = g * STEP + t
            held[q, b, :SPAN] = zero8
            held[q, b, SPAN : SPAN + box] = row
            held[q, b, SPAN + box :] = zero8
            acc[q, b] = jnp.zeros((box + 2 * SPAN, LANES), F32)
        return 0

    lax.fori_loop(0, n_cubes // 2 * steps, unpack, 0)
    active = counts[0]

    def group(g, _):
        slots = []
        for p in range(2):
            slot = jnp.minimum(2 * g + p, active - 1)
            live = (2 * g + p < active).astype(F32)
            first, second = pairs[slot, 0], pairs[slot, 1]
            section = second // region_size
            member = second - section * region_size
            ci, cj = id_of(first, 1), id_of(member, section)
            e = [corners[cj, d] - corners[ci, d] for d in range(3)]
            i, j = place_of(first, 1), place_of(member, section)
            slots.append((live, i, j, e))

        def forward(c, _):
            rhos = []
            for t in range(STEP):
                b = c * STEP + t
                us, phis = [], []
                for p, (live, i, j, e) in enumerate(slots):
                    phi = pltpu.roll(held[i // 2, b, SPAN : SPAN + box], HALF * ((p + i) % 2), 1)
                    phis.append(phi * live)
                    bj = b - e[1]
                    inside = jnp.logical_and(bj >= 0, bj < box).astype(F32)
                    at = jnp.clip(bj, 0, box - 1)
                    u = held[j // 2, at, pl.ds(SPAN - e[0], box)]
                    amount = lax.rem(e[2] + HALF * (p + j % 2) + LANES, LANES)
                    us.append(pltpu.roll(u, amount, 1) * inside)
                u = jnp.where(lane < HALF, us[0], us[1])
                phi = jnp.where(lane < HALF, phis[0], phis[1])
                u_all[b] = u
                phi_all[b] = phi
                rhos.append(u * phi)
            y = lane_transform(lanes_ref[...], jnp.concatenate(rhos, axis=0))
            for t in range(0, STEP, 2):
                pair = row_transform(rows_ref[...], [y[box * t : box * (t + 1)], y[box * (t + 1) : box * (t + 2)]])
                start = pl.multiple_of((c * STEP + t) * box, 8)
                work[pl.ds(start, box)] = pair[0]
                work[pl.ds(start + box, box)] = pair[1]
            return 0

        lax.fori_loop(0, steps, forward, 0)

        def middle(c, _):
            for h in range(0, STEP, 2):
                a = c * STEP + h
                xs = [work[pl.ds(a + k, box, stride=box)] for k in range(2)]
                ys = row_transform(rows_ref[...], xs)
                zs = row_transform(rows_ref[...], [ys[k] * green[a + k] for k in range(2)])
                for k in range(2):
                    work[pl.ds(a + k, box, stride=box)] = zs[k]
            return 0

        lax.fori_loop(0, steps, middle, 0)

        def backward(c, _):
            xs = []
            for t in range(0, STEP, 2):
                start = pl.multiple_of((c * STEP + t) * box, 8)
                xs.extend(row_transform(rows_ref[...], [work[pl.ds(start, box)], work[pl.ds(start + box, box)]]))
            v_all = lane_transform(lanes_ref[...], jnp.concatenate(xs, axis=0))
            for t in range(STEP):
                b = c * STEP + t
                v = v_all[box * t : box * (t + 1)]
                vu = v * u_all[b]
                vp = v * phi_all[b]
                for p, (live, i, j, e) in enumerate(slots):
                    half = lane < HALF if p == 0 else lane >= HALF
                    acc[i // 2, b, SPAN : SPAN + box] += pltpu.roll(
                        jnp.where(half, vu, 0.0), HALF * ((p + i) % 2), 1
                    )
                    bj = b - e[1]
                    inside = jnp.logical_and(bj >= 0, bj < box).astype(F32)
                    at = jnp.clip(bj, 0, box - 1)
                    amount = lax.rem(HALF * (p + j % 2) + LANES - e[2], LANES)
                    acc[j // 2, at, pl.ds(SPAN - e[0], box)] += (
                        pltpu.roll(jnp.where(half, vp, 0.0), amount, 1) * inside
                    )
            return 0

        lax.fori_loop(0, steps, backward, 0)
        return 0

    lax.fori_loop(0, (active + 1) // 2, group, 0)

    def pack(item, _):
        q, g = item // steps, item % steps
        rows = [acc[q, g * STEP + t, SPAN : SPAN + box] for t in range(STEP)]
        start = pl.multiple_of(g * (box * STEP), LANES)
        for h in range(2):
            for k, block in enumerate(pack_blocks(box, rows, HALF * h, lane)):
                out[2 * q + h, :, pl.ds(start + LANES * k, LANES)] = block.astype(BF16)
        return 0

    lax.fori_loop(0, n_cubes // 2 * steps, pack, 0)


def gram_kernel(dims, corners, cubes, mid, above, below, exchange, gram, held):
    box, own, blocks, regions = dims
    region_size = own * blocks
    box_index, block_index = lax.axis_index("box"), lax.axis_index("orb")
    lane = lane_ids(box)
    steps = box // STEP
    zero8 = jnp.zeros((SPAN, LANES), F32)

    def id_of(member):
        return ((member // own) * regions + box_index) * own + member % own

    def unpack(item, _):
        q, g = item // steps, item % steps
        pieces = []
        for h in range(2):
            member = 2 * q + h
            pieces.append(load_blocks(box, cubes, (member // own, member % own), g))
        for t, row in enumerate(unpack_pair(box, pieces[0], pieces[1], lane)):
            b = g * STEP + t
            held[q, b, :SPAN] = zero8
            held[q, b, SPAN : SPAN + box] = row
            held[q, b, SPAN + box :] = zero8
        return 0

    lax.fori_loop(0, region_size // 2 * steps, unpack, 0)

    for col in range(own):
        me = id_of(block_index * own + col)
        shifts = []
        for k in range(region_size):
            ck = id_of(k)
            shifts.append([corners[ck, d] - corners[me, d] for d in range(3)])

        def step(g, sums):
            blocks_f = [
                a + b + c
                for a, b, c in zip(
                    load_blocks(box, mid, (col,), g),
                    load_blocks(box, above, (col,), g),
                    load_blocks(box, below, (col,), g),
                )
            ]
            start = pl.multiple_of(g * (box * STEP), LANES)
            for k, block in enumerate(blocks_f):
                exchange[col, :, pl.ds(start + LANES * k, LANES)] = block.astype(BF16)
            sums = list(sums)
            for t, (x, off) in enumerate(unpack_step(box, blocks_f, lane)):
                b = g * STEP + t
                x = pltpu.roll(x, (-off) % LANES, 1) if off else x
                x = jnp.where(lane < box, x, 0.0)
                for k in range(region_size):
                    e = shifts[k]
                    bj = b - e[1]
                    inside = jnp.logical_and(bj >= 0, bj < box).astype(F32)
                    at = jnp.clip(bj, 0, box - 1)
                    u = held[k // 2, at, pl.ds(SPAN - e[0], box)]
                    amount = lax.rem(e[2] + HALF * (k % 2) + LANES, LANES)
                    part = pltpu.roll(u, amount, 1) * x * inside
                    total = part[:8]
                    for r in range(8, box, 8):
                        total = total + part[r : r + 8]
                    sums[k] = sums[k] + total
            return tuple(sums)

        sums = lax.fori_loop(0, steps, step, tuple(jnp.zeros((8, LANES), F32) for _ in range(region_size)))
        for k in range(region_size):
            gram[k, col] = jnp.sum(sums[k]) * (1.0 / box**3)


def per_device(orbitals, corners, pairs, counts):
    own, box, plane = orbitals.shape
    blocks = lax.axis_size("orb")
    regions = lax.axis_size("box")
    region_size = own * blocks
    n_cubes = 3 * region_size
    dims = (box, own, blocks, regions)
    up = [(i, (i + 1) % regions) for i in range(regions)]
    down = [((i + 1) % regions, i) for i in range(regions)]
    mine = jnp.concatenate(
        [lax.ppermute(orbitals, "box", up), orbitals, lax.ppermute(orbitals, "box", down)], axis=0
    )
    gathered = lax.all_gather(mine, "orb", axis=0, tiled=True)
    rows, lanes, green = tables(box)
    smem = pl.BlockSpec(memory_space=pltpu.SMEM)
    vmem = pl.BlockSpec(memory_space=pltpu.VMEM)
    padded = (box, box + 2 * SPAN, LANES)
    totals = pl.pallas_call(
        functools.partial(pair_kernel, dims),
        out_shape=jax.ShapeDtypeStruct((n_cubes, box, plane), BF16),
        in_specs=[smem, smem, smem, vmem, vmem, vmem, vmem],
        out_specs=vmem,
        scratch_shapes=[
            pltpu.VMEM((n_cubes // 2, *padded), F32),
            pltpu.VMEM((n_cubes // 2, *padded), F32),
            pltpu.VMEM((box * box, LANES), F32),
            pltpu.VMEM((box, box, LANES), F32),
            pltpu.VMEM((box, box, LANES), F32),
        ],
        compiler_params=pltpu.CompilerParams(vmem_limit_bytes=60 * 2**20),
        name="pair_potentials",
    )(corners, pairs, counts, gathered, jnp.asarray(rows), jnp.asarray(lanes), jnp.asarray(green))
    reduced = lax.psum_scatter(totals, "orb", scatter_dimension=0, tiled=True)
    above = lax.ppermute(reduced[:own], "box", down)
    below = lax.ppermute(reduced[2 * own :], "box", up)
    region = gathered.reshape(blocks, 3, own, box, plane)[:, 1]
    exchange, columns = pl.pallas_call(
        functools.partial(gram_kernel, dims),
        out_shape=(
            jax.ShapeDtypeStruct((own, box, plane), BF16),
            jax.ShapeDtypeStruct((region_size, own), F32),
        ),
        in_specs=[smem, vmem, vmem, vmem, vmem],
        out_specs=(vmem, smem),
        scratch_shapes=[pltpu.VMEM((region_size // 2, *padded), F32)],
        compiler_params=pltpu.CompilerParams(vmem_limit_bytes=40 * 2**20),
        name="gram_columns",
    )(corners, region, reduced[own : 2 * own], above, below)
    gram = lax.all_gather(columns, "orb", axis=1, tiled=True)
    return exchange, gram[None]


def solution(mesh):
    placed = (P(("orb", "box"), None, None), P(), P(("orb", "box"), None), P(("orb", "box")))
    return jax.shard_map(
        per_device,
        mesh=mesh,
        in_specs=placed,
        out_specs=(P(("orb", "box"), None, None), P("box", None, None)),
        check_vma=False,
    )
```

```python
import functools
import math

import jax
import jax.numpy as jnp
import ml_dtypes
import numpy as np
from jax import lax
from jax.experimental import pallas as pl
from jax.experimental.pallas import tpu as pltpu
from jax.sharding import PartitionSpec as P

SPAN = 8
SCREEN = 0.5
HALF = 64
LANES = 128
STEP = 8
PIECE = 16
F32 = jnp.float32
BF16 = jnp.bfloat16


def tables(box):
    n = np.arange(box)
    angle = (n[:, None] * n[None, :] % box) * (2.0 * math.pi / box)
    cas = np.cos(angle) + np.sin(angle)
    hi = cas.astype(ml_dtypes.bfloat16)
    lo = (cas - hi.astype(np.float64)).astype(ml_dtypes.bfloat16)
    rows = np.concatenate([hi, hi, lo], axis=1)
    lanes = np.zeros((2 * LANES, 2 * LANES), ml_dtypes.bfloat16)
    for p in range(2):
        s = slice(HALF * p, HALF * p + box)
        t = slice(LANES + HALF * p, LANES + HALF * p + box)
        lanes[s, s] = hi
        lanes[t, s] = hi
        lanes[s, t] = lo
    k = np.minimum(n, box - n) * (2.0 * math.pi / box)
    k2 = k * k
    g = -1.0 / (k2[:, None, None] + k2[None, :, None] + k2[None, None, :] + SCREEN) / box**3
    green = np.zeros((box, box, LANES), np.float32)
    for p in range(2):
        green[:, :, HALF * p : HALF * p + box] = g
    return rows, lanes, green


def lane_ids(rows):
    return lax.broadcasted_iota(jnp.int32, (rows, LANES), 1)


def unpack_step(box, blocks, lane):
    out = []
    for t in range(STEP):
        start = box * t
        blk, off = start // LANES, start % LANES
        x = blocks[blk]
        if off + box > LANES:
            x = jnp.where(lane >= off, x, blocks[blk + 1])
        out.append((x, off))
    return out


def unpack_pair(box, first, second, lane):
    out = []
    for (x, off), (y, _) in zip(unpack_step(box, first, lane), unpack_step(box, second, lane)):
        a = pltpu.roll(x, (-off) % LANES, 1) if off else x
        b = pltpu.roll(y, (HALF - off) % LANES, 1) if off != HALF else y
        both = jnp.where(lane < HALF, a, b)
        out.append(jnp.where(lane % HALF < box, both, 0.0))
    return out


def pack_blocks(box, rows, shift, lane):
    n_blocks = box * STEP // LANES
    blocks = [None] * n_blocks
    for t in range(STEP):
        start = box * t
        amount = (start - shift) % LANES
        x = pltpu.roll(rows[t], amount, 1) if amount else rows[t]
        for blk in range(start // LANES, (start + box - 1) // LANES + 1):
            lo = start - blk * LANES
            if blocks[blk] is None:
                blocks[blk] = x
            else:
                blocks[blk] = jnp.where(lane >= max(lo, 0), x, blocks[blk])
    return blocks


def load_blocks(box, ref, lead, g):
    width = box * STEP
    start = pl.multiple_of(g * width, LANES)
    return [
        ref[(*lead, slice(None), pl.ds(start + LANES * k, LANES))].astype(F32)
        for k in range(width // LANES)
    ]


def split_rows(x):
    hi = x.astype(BF16)
    lo = (x - hi.astype(F32)).astype(BF16)
    return hi, lo


def row_transform(t_rows, xs):
    x = jnp.concatenate(xs, axis=1)
    hi, lo = split_rows(x)
    stacked = jnp.concatenate([hi, lo, hi], axis=0)
    y = jnp.dot(t_rows, stacked, preferred_element_type=F32)
    return y[:, :LANES], y[:, LANES:]


def lane_transform(t_lanes, x):
    hi, lo = split_rows(x)
    y = jnp.dot(jnp.concatenate([hi, lo], axis=1), t_lanes, preferred_element_type=F32)
    return y[:, :LANES] + y[:, LANES:]


def pair_kernel(
    dims, corners, meta, cubes, rows_ref, lanes_ref, green, out, held, acc, work, u_all, phi_all
):
    box, own, blocks, regions = dims
    region_size = own * blocks
    n_cubes = 3 * region_size
    box_index, rank = lax.axis_index("box"), lax.axis_index("orb")
    lane = lane_ids(box)
    steps = box // STEP
    zero8 = jnp.zeros((SPAN, LANES), F32)

    def place_of(member, section):
        return (member // own) * (3 * own) + section * own + member % own

    def id_of(member, section):
        neighbour = lax.rem(box_index + section - 1 + regions, regions)
        return ((member // own) * regions + neighbour) * own + member % own

    def unpack(item, _):
        q, g = item // steps, item % steps
        first = load_blocks(box, cubes, (2 * q,), g)
        second = load_blocks(box, cubes, (2 * q + 1,), g)
        for t, row in enumerate(unpack_pair(box, first, second, lane)):
            b = g * STEP + t
            held[q, b, :SPAN] = zero8
            held[q, b, SPAN : SPAN + box] = row
            held[q, b, SPAN + box :] = zero8
            acc[q, b] = jnp.zeros((box + 2 * SPAN, LANES), F32)
        return 0

    lax.fori_loop(0, n_cubes // 2 * steps, unpack, 0)
    ends = [meta[0, 2, 0]]
    for o in range(1, blocks):
        ends.append(ends[-1] + meta[o, 2, 0])
    active = (ends[-1] - rank + blocks - 1) // blocks

    def slot_of(turn):
        item = rank + blocks * turn
        device, slot = 0, item
        for end in ends[:-1]:
            past = item >= end
            device = device + past.astype(jnp.int32)
            slot = jnp.where(past, item - end, slot)
        return meta[device, 0, slot], meta[device, 1, slot]

    def group(g, _):
        slots = []
        for p in range(2):
            live = (2 * g + p < active).astype(F32)
            first, second = slot_of(jnp.minimum(2 * g + p, active - 1))
            section = second // region_size
            member = second - section * region_size
            ci, cj = id_of(first, 1), id_of(member, section)
            e = [corners[cj, d] - corners[ci, d] for d in range(3)]
            i, j = place_of(first, 1), place_of(member, section)
            slots.append((live, i, j, e))

        def forward(c, _):
            rhos = []
            for t in range(STEP):
                b = c * STEP + t
                us, phis = [], []
                for p, (live, i, j, e) in enumerate(slots):
                    phi = pltpu.roll(held[i // 2, b, SPAN : SPAN + box], HALF * ((p + i) % 2), 1)
                    phis.append(phi * live)
                    bj = b - e[1]
                    inside = jnp.logical_and(bj >= 0, bj < box).astype(F32)
                    at = jnp.clip(bj, 0, box - 1)
                    u = held[j // 2, at, pl.ds(SPAN - e[0], box)]
                    amount = lax.rem(e[2] + HALF * (p + j % 2) + LANES, LANES)
                    us.append(pltpu.roll(u, amount, 1) * inside)
                u = jnp.where(lane < HALF, us[0], us[1])
                phi = jnp.where(lane < HALF, phis[0], phis[1])
                u_all[b] = u
                phi_all[b] = phi
                rhos.append(u * phi)
            y = lane_transform(lanes_ref[...], jnp.concatenate(rhos, axis=0))
            for t in range(0, STEP, 2):
                pair = row_transform(rows_ref[...], [y[box * t : box * (t + 1)], y[box * (t + 1) : box * (t + 2)]])
                start = pl.multiple_of((c * STEP + t) * box, 8)
                work[pl.ds(start, box)] = pair[0]
                work[pl.ds(start + box, box)] = pair[1]
            return 0

        lax.fori_loop(0, steps, forward, 0)

        def middle(c, _):
            for h in range(0, STEP, 2):
                a = c * STEP + h
                xs = [work[pl.ds(a + k, box, stride=box)] for k in range(2)]
                ys = row_transform(rows_ref[...], xs)
                zs = row_transform(rows_ref[...], [ys[k] * green[a + k] for k in range(2)])
                for k in range(2):
                    work[pl.ds(a + k, box, stride=box)] = zs[k]
            return 0

        lax.fori_loop(0, steps, middle, 0)

        def backward(c, _):
            xs = []
            for t in range(0, STEP, 2):
                start = pl.multiple_of((c * STEP + t) * box, 8)
                xs.extend(row_transform(rows_ref[...], [work[pl.ds(start, box)], work[pl.ds(start + box, box)]]))
            v_all = lane_transform(lanes_ref[...], jnp.concatenate(xs, axis=0))
            for t in range(STEP):
                b = c * STEP + t
                v = v_all[box * t : box * (t + 1)]
                vu = v * u_all[b]
                vp = v * phi_all[b]
                for p, (live, i, j, e) in enumerate(slots):
                    half = lane < HALF if p == 0 else lane >= HALF
                    acc[i // 2, b, SPAN : SPAN + box] += pltpu.roll(
                        jnp.where(half, vu, 0.0), HALF * ((p + i) % 2), 1
                    )
                    bj = b - e[1]
                    inside = jnp.logical_and(bj >= 0, bj < box).astype(F32)
                    at = jnp.clip(bj, 0, box - 1)
                    amount = lax.rem(HALF * (p + j % 2) + LANES - e[2], LANES)
                    acc[j // 2, at, pl.ds(SPAN - e[0], box)] += (
                        pltpu.roll(jnp.where(half, vp, 0.0), amount, 1) * inside
                    )
            return 0

        lax.fori_loop(0, steps, backward, 0)
        return 0

    lax.fori_loop(0, (active + 1) // 2, group, 0)

    def pack(item, _):
        q, g = item // steps, item % steps
        rows = [acc[q, g * STEP + t, SPAN : SPAN + box] for t in range(STEP)]
        start = pl.multiple_of(g * (box * STEP), LANES)
        for h in range(2):
            for k, block in enumerate(pack_blocks(box, rows, HALF * h, lane)):
                out[2 * q + h, :, pl.ds(start + LANES * k, LANES)] = block.astype(BF16)
        return 0

    lax.fori_loop(0, n_cubes // 2 * steps, pack, 0)


def partners(blocks, regions):
    me, region = lax.axis_index("orb"), lax.axis_index("box")
    up, down = lax.rem(region + 1, regions), lax.rem(region + regions - 1, regions)
    mate = me + 1 - 2 * lax.rem(me, 2)
    peers = [lax.rem(me + 2 * d, blocks) for d in range(1, blocks // 2)]
    mates_peers = [lax.rem(mate + 2 * d, blocks) for d in range(1, blocks // 2)]
    others = [lax.rem(me + d, blocks) for d in range(1, blocks)]
    return me, region, up, down, mate, peers, mates_peers, others


def meet(me, region, up, down, others):
    barrier = pltpu.get_barrier_semaphore()
    devices = [(me, up), (me, down)] + [(o, region) for o in others]
    for device in devices:
        pl.semaphore_signal(barrier, inc=1, device_id=device, device_id_type=pl.DeviceIdType.MESH)
    pl.semaphore_wait(barrier, len(devices))


def remote(src, dst, send, recv, device):
    return pltpu.make_async_remote_copy(
        src_ref=src, dst_ref=dst, send_sem=send, recv_sem=recv, device_id=device,
        device_id_type=pl.DeviceIdType.MESH,
    )


def gather_kernel(dims, mine, meta, out, meta_out, send, recv, meta_send, meta_recv):
    box, own, blocks, regions = dims
    me, region, up, down, mate, peers, mates_peers, others = partners(blocks, regions)
    pieces = box // PIECE
    meet(me, region, up, down, others)
    sent = []

    def piece(o, s, k):
        return out.at[o, pl.ds(s * own, own), pl.ds(PIECE * k, PIECE)]

    def push(src, o, s, k, device):
        copy = remote(src, piece(o, s, k), send.at[len(sent)], recv.at[o, s, k], device)
        copy.start()
        sent.append(copy)

    def arrived(o, s, k):
        ref = piece(o, s, k)
        remote(ref, ref, send.at[0], recv.at[o, s, k], (mate, region)).wait_recv()

    for k in range(pieces):
        src = mine.at[:, pl.ds(PIECE * k, PIECE)]
        push(src, me, 0, k, (me, up))
        push(src, me, 2, k, (me, down))
    metas = []
    for n, o in enumerate(others):
        copy = remote(meta, meta_out.at[me], meta_send.at[n], meta_recv.at[me], (o, region))
        copy.start()
        metas.append(copy)
    for k in range(pieces):
        src = mine.at[:, pl.ds(PIECE * k, PIECE)]
        for peer in peers:
            push(src, me, 1, k, (peer, region))
        push(src, me, 1, k, (mate, region))
    out[me, pl.ds(own, own)] = mine[...]
    meta_out[me] = meta[...]
    for k in range(pieces):
        for s in (0, 2):
            arrived(me, s, k)
            for peer in peers:
                push(piece(me, s, k), me, s, k, (peer, region))
            push(piece(me, s, k), me, s, k, (mate, region))
        for peer in peers:
            arrived(peer, 1, k)
            push(piece(peer, 1, k), peer, 1, k, (mate, region))
    for k in range(pieces):
        for s in (0, 2):
            for peer in peers:
                arrived(peer, s, k)
                push(piece(peer, s, k), peer, s, k, (mate, region))
    for o in [mate] + mates_peers:
        for s in range(3):
            for k in range(pieces):
                arrived(o, s, k)
    for o in others:
        remote(meta, meta_out.at[o], meta_send.at[0], meta_recv.at[o], (mate, region)).wait_recv()
    for copy in sent + metas:
        copy.wait_send()


def reduce_kernel(
    dims, corners, cubes, totals, exchange, gram,
    held, mate_in, peer_out, peer_in, side_out, side_in, mid, columns,
    mate_send, mate_recv, peer_send, peer_recv, side_send, side_recv, col_send, col_recv,
):
    box, own, blocks, regions = dims
    region_size = own * blocks
    me, region, up, down, mate, peers, mates_peers, others = partners(blocks, regions)
    pieces = box // PIECE
    lane = lane_ids(box)
    steps = box // STEP
    zero8 = jnp.zeros((SPAN, LANES), F32)
    order = (0, 2, 1)
    meet(me, region, up, down, others)

    def part(ref, o, s, k):
        return ref.at[o, pl.ds(s * own, own), pl.ds(PIECE * k, PIECE)]

    def value(ref, o, s, k):
        return ref[o, pl.ds(s * own, own), pl.ds(PIECE * k, PIECE)].astype(F32)

    sent = []
    for t in mates_peers + [mate]:
        for s in order:
            for k in range(pieces):
                copy = remote(
                    part(totals, t, s, k), part(mate_in, t // 2, s, k),
                    mate_send.at[t // 2, s, k], mate_recv.at[t // 2, s, k], (mate, region),
                )
                copy.start()
                sent.append(copy)

    def from_mate(t, s, k):
        ref = part(mate_in, t // 2, s, k)
        remote(ref, ref, mate_send.at[0, 0, 0], mate_recv.at[t // 2, s, k], (mate, region)).wait_recv()

    for s in order:
        for k in range(pieces):
            for t in peers:
                from_mate(t, s, k)
                both = value(totals, t, s, k) + value(mate_in, t // 2, s, k)
                peer_out[t // 2, pl.ds(s * own, own), pl.ds(PIECE * k, PIECE)] = both.astype(BF16)
                copy = remote(
                    part(peer_out, t // 2, s, k), part(peer_in, me // 2, s, k),
                    peer_send.at[t // 2, s, k], peer_recv.at[me // 2, s, k], (t, region),
                )
                copy.start()
                sent.append(copy)

    def id_of(member):
        return ((member // own) * regions + region) * own + member % own

    def unpack(item, _):
        q, g = item // steps, item % steps
        halves = []
        for h in range(2):
            member = 2 * q + h
            halves.append(load_blocks(box, cubes, (member // own, own + member % own), g))
        for t, row in enumerate(unpack_pair(box, halves[0], halves[1], lane)):
            b = g * STEP + t
            held[q, b, :SPAN] = zero8
            held[q, b, SPAN : SPAN + box] = row
            held[q, b, SPAN + box :] = zero8
        return 0

    lax.fori_loop(0, region_size // 2 * steps, unpack, 0)

    for s in order:
        for k in range(pieces):
            from_mate(me, s, k)
            total = value(totals, me, s, k) + value(mate_in, me // 2, s, k)
            for t in peers:
                ref = part(peer_in, t // 2, s, k)
                remote(ref, ref, peer_send.at[0, 0, 0], peer_recv.at[t // 2, s, k], (t, region)).wait_recv()
                total = total + value(peer_in, t // 2, s, k)
            if s == 1:
                mid[:, pl.ds(PIECE * k, PIECE)] = total
                continue
            side = s // 2
            side_out[side, :, pl.ds(PIECE * k, PIECE)] = total.astype(BF16)
            copy = remote(
                side_out.at[side, :, pl.ds(PIECE * k, PIECE)], side_in.at[side, :, pl.ds(PIECE * k, PIECE)],
                side_send.at[side, k], side_recv.at[side, k], (me, down if s == 0 else up),
            )
            copy.start()
            sent.append(copy)
    for k in range(pieces):
        for side in range(2):
            ref = side_in.at[side, :, pl.ds(PIECE * k, PIECE)]
            remote(ref, ref, side_send.at[0, 0], side_recv.at[side, k], (me, up)).wait_recv()

    row8 = lax.broadcasted_iota(jnp.int32, (8, LANES), 0)
    lane8 = lane_ids(8)
    tile = jnp.zeros((8, LANES), F32)
    for col in range(own):
        mine = id_of(me * own + col)
        shifts = []
        for k in range(region_size):
            ck = id_of(k)
            shifts.append([corners[ck, d] - corners[mine, d] for d in range(3)])

        def step(g, sums):
            blocks_f = [
                a + b + c
                for a, b, c in zip(
                    load_blocks(box, mid, (col,), g),
                    load_blocks(box, side_in, (0, col), g),
                    load_blocks(box, side_in, (1, col), g),
                )
            ]
            start = pl.multiple_of(g * (box * STEP), LANES)
            for k, block in enumerate(blocks_f):
                exchange[col, :, pl.ds(start + LANES * k, LANES)] = block.astype(BF16)
            sums = list(sums)
            for t, (x, off) in enumerate(unpack_step(box, blocks_f, lane)):
                b = g * STEP + t
                x = pltpu.roll(x, (-off) % LANES, 1) if off else x
                x = jnp.where(lane < box, x, 0.0)
                for k in range(region_size):
                    e = shifts[k]
                    bj = b - e[1]
                    inside = jnp.logical_and(bj >= 0, bj < box).astype(F32)
                    at = jnp.clip(bj, 0, box - 1)
                    u = held[k // 2, at, pl.ds(SPAN - e[0], box)]
                    amount = lax.rem(e[2] + HALF * (k % 2) + LANES, LANES)
                    product = pltpu.roll(u, amount, 1) * x * inside
                    total = product[:8]
                    for r in range(8, box, 8):
                        total = total + product[r : r + 8]
                    sums[k] = sums[k] + total
            return tuple(sums)

        sums = lax.fori_loop(0, steps, step, tuple(jnp.zeros((8, LANES), F32) for _ in range(region_size)))
        for k in range(region_size):
            here = jnp.logical_and(row8 == k, lane8 == col)
            tile = jnp.where(here, jnp.sum(sums[k]) * (1.0 / box**3), tile)
    columns[me] = tile
    for n, o in enumerate(others):
        copy = remote(columns.at[me], columns.at[me], col_send.at[n], col_recv.at[me], (o, region))
        copy.start()
        sent.append(copy)
    for o in others:
        remote(columns.at[o], columns.at[o], col_send.at[0], col_recv.at[o], (mate, region)).wait_recv()
    whole = columns[0]
    for o in range(1, blocks):
        whole = whole + pltpu.roll(columns[o], o * own, 1)
    gram[0] = whole[:region_size, :region_size]
    for copy in sent:
        copy.wait_send()


def per_device(orbitals, corners, pairs, counts):
    own, box, plane = orbitals.shape
    blocks = lax.axis_size("orb")
    regions = lax.axis_size("box")
    region_size = own * blocks
    n_cubes = 3 * region_size
    dims = (box, own, blocks, regions)
    slots = pairs.shape[0]
    pieces = box // PIECE
    smem = pl.BlockSpec(memory_space=pltpu.SMEM)
    vmem = pl.BlockSpec(memory_space=pltpu.VMEM)
    dma = pltpu.SemaphoreType.DMA
    meta = jnp.stack([pairs[:, 0], pairs[:, 1], jnp.broadcast_to(counts[:1], (slots,))])
    meta = jnp.pad(meta, ((0, 5), (0, LANES - slots)))
    sends = pieces * (2 + 3 * (blocks - 1))
    gathered, metas = pl.pallas_call(
        functools.partial(gather_kernel, dims),
        out_shape=(
            jax.ShapeDtypeStruct((blocks, 3 * own, box, plane), BF16),
            jax.ShapeDtypeStruct((blocks, 8, LANES), jnp.int32),
        ),
        in_specs=[vmem, vmem],
        out_specs=(vmem, vmem),
        scratch_shapes=[
            dma((sends,)), dma((blocks, 3, pieces)), dma((blocks - 1,)), dma((blocks,)),
        ],
        compiler_params=pltpu.CompilerParams(
            collective_id=0, has_side_effects=True, vmem_limit_bytes=24 * 2**20
        ),
        name="gather_window",
    )(orbitals, meta)
    rows, lanes, green = tables(box)
    padded = (box, box + 2 * SPAN, LANES)
    totals = pl.pallas_call(
        functools.partial(pair_kernel, dims),
        out_shape=jax.ShapeDtypeStruct((n_cubes, box, plane), BF16),
        in_specs=[smem, smem, vmem, vmem, vmem, vmem],
        out_specs=vmem,
        scratch_shapes=[
            pltpu.VMEM((n_cubes // 2, *padded), F32),
            pltpu.VMEM((n_cubes // 2, *padded), F32),
            pltpu.VMEM((box * box, LANES), F32),
            pltpu.VMEM((box, box, LANES), F32),
            pltpu.VMEM((box, box, LANES), F32),
        ],
        compiler_params=pltpu.CompilerParams(vmem_limit_bytes=60 * 2**20),
        name="pair_potentials",
    )(
        corners, metas, gathered.reshape(n_cubes, box, plane),
        jnp.asarray(rows), jnp.asarray(lanes), jnp.asarray(green),
    )
    chips = blocks // 2
    wide = (chips, 3 * own, box, plane)
    exchange, gram = pl.pallas_call(
        functools.partial(reduce_kernel, dims),
        out_shape=(
            jax.ShapeDtypeStruct((own, box, plane), BF16),
            jax.ShapeDtypeStruct((1, region_size, region_size), F32),
        ),
        in_specs=[smem, vmem, vmem],
        out_specs=(vmem, vmem),
        scratch_shapes=[
            pltpu.VMEM((region_size // 2, *padded), F32),
            pltpu.VMEM(wide, BF16),
            pltpu.VMEM(wide, BF16),
            pltpu.VMEM(wide, BF16),
            pltpu.VMEM((2, own, box, plane), BF16),
            pltpu.VMEM((2, own, box, plane), BF16),
            pltpu.VMEM((own, box, plane), F32),
            pltpu.VMEM((blocks, 8, LANES), F32),
            dma((chips, 3, pieces)), dma((chips, 3, pieces)),
            dma((chips, 3, pieces)), dma((chips, 3, pieces)),
            dma((2, pieces)), dma((2, pieces)),
            dma((blocks - 1,)), dma((blocks,)),
        ],
        compiler_params=pltpu.CompilerParams(
            collective_id=1, has_side_effects=True, vmem_limit_bytes=48 * 2**20
        ),
        name="reduce_and_gram",
    )(corners, gathered, totals.reshape(blocks, 3 * own, box, plane))
    return exchange, gram


def solution(mesh):
    placed = (P(("orb", "box"), None, None), P(), P(("orb", "box"), None), P(("orb", "box")))
    return jax.shard_map(
        per_device,
        mesh=mesh,
        in_specs=placed,
        out_specs=(P(("orb", "box"), None, None), P("box", None, None)),
        check_vma=False,
    )
```

```python
import functools
import math

import jax
import jax.numpy as jnp
import ml_dtypes
import numpy as np
from jax import lax
from jax.experimental import pallas as pl
from jax.experimental.pallas import tpu as pltpu
from jax.sharding import PartitionSpec as P

SPAN = 8
SCREEN = 0.5
HALF = 64
LANES = 128
STEP = 8
PIECE = 16
F32 = jnp.float32
BF16 = jnp.bfloat16


def tables(box):
    n = np.arange(box)
    angle = (n[:, None] * n[None, :] % box) * (2.0 * math.pi / box)
    cas = np.cos(angle) + np.sin(angle)
    hi = cas.astype(ml_dtypes.bfloat16)
    lo = (cas - hi.astype(np.float64)).astype(ml_dtypes.bfloat16)
    rows = np.concatenate([hi, hi, lo], axis=1)
    lanes = np.zeros((2 * LANES, 2 * LANES), ml_dtypes.bfloat16)
    for p in range(2):
        s = slice(HALF * p, HALF * p + box)
        t = slice(LANES + HALF * p, LANES + HALF * p + box)
        lanes[s, s] = hi
        lanes[t, s] = hi
        lanes[s, t] = lo
    k = np.minimum(n, box - n) * (2.0 * math.pi / box)
    k2 = k * k
    g = -1.0 / (k2[:, None, None] + k2[None, :, None] + k2[None, None, :] + SCREEN) / box**3
    green = np.zeros((box, box, LANES), np.float32)
    for p in range(2):
        green[:, :, HALF * p : HALF * p + box] = g
    return rows, lanes, green


def lane_ids(rows):
    return lax.broadcasted_iota(jnp.int32, (rows, LANES), 1)


def unpack_step(box, blocks, lane):
    out = []
    for t in range(STEP):
        start = box * t
        blk, off = start // LANES, start % LANES
        x = blocks[blk]
        if off + box > LANES:
            x = jnp.where(lane >= off, x, blocks[blk + 1])
        out.append((x, off))
    return out


def unpack_pair(box, first, second, lane):
    out = []
    for (x, off), (y, _) in zip(unpack_step(box, first, lane), unpack_step(box, second, lane)):
        a = pltpu.roll(x, (-off) % LANES, 1) if off else x
        b = pltpu.roll(y, (HALF - off) % LANES, 1) if off != HALF else y
        both = jnp.where(lane < HALF, a, b)
        out.append(jnp.where(lane % HALF < box, both, 0.0))
    return out


def pack_blocks(box, rows, shift, lane):
    n_blocks = box * STEP // LANES
    blocks = [None] * n_blocks
    for t in range(STEP):
        start = box * t
        amount = (start - shift) % LANES
        x = pltpu.roll(rows[t], amount, 1) if amount else rows[t]
        for blk in range(start // LANES, (start + box - 1) // LANES + 1):
            lo = start - blk * LANES
            if blocks[blk] is None:
                blocks[blk] = x
            else:
                blocks[blk] = jnp.where(lane >= max(lo, 0), x, blocks[blk])
    return blocks


def load_blocks(box, ref, lead, g):
    width = box * STEP
    start = g * width if isinstance(g, int) else pl.multiple_of(g * width, LANES)
    return [
        ref[(*lead, slice(None), pl.ds(start + LANES * k, LANES))].astype(F32)
        for k in range(width // LANES)
    ]


def split_rows(x):
    hi = x.astype(BF16)
    lo = (x - hi.astype(F32)).astype(BF16)
    return hi, lo


def row_transform(t_rows, xs):
    x = jnp.concatenate(xs, axis=1)
    hi, lo = split_rows(x)
    stacked = jnp.concatenate([hi, lo, hi], axis=0)
    y = jnp.dot(t_rows, stacked, preferred_element_type=F32)
    return y[:, :LANES], y[:, LANES:]


def lane_transform(t_lanes, x):
    hi, lo = split_rows(x)
    y = jnp.dot(jnp.concatenate([hi, lo], axis=1), t_lanes, preferred_element_type=F32)
    return y[:, :LANES] + y[:, LANES:]


def pair_kernel(
    dims, corners, meta, cubes, rows_ref, lanes_ref, green, out, held, acc, work, turned, u_all, phi_all
):
    box, own, blocks, regions = dims
    region_size = own * blocks
    n_cubes = 3 * region_size
    box_index, rank = lax.axis_index("box"), lax.axis_index("orb")
    lane = lane_ids(box)
    steps = box // STEP
    zero8 = jnp.zeros((SPAN, LANES), F32)

    def place_of(member, section):
        return (member // own) * (3 * own) + section * own + member % own

    def id_of(member, section):
        neighbour = lax.rem(box_index + section - 1 + regions, regions)
        return ((member // own) * regions + neighbour) * own + member % own

    def unpack(item, _):
        q, g = item // steps, item % steps
        first = load_blocks(box, cubes, (2 * q,), g)
        second = load_blocks(box, cubes, (2 * q + 1,), g)
        for t, row in enumerate(unpack_pair(box, first, second, lane)):
            b = g * STEP + t
            held[q, b, :SPAN] = zero8
            held[q, b, SPAN : SPAN + box] = row
            held[q, b, SPAN + box :] = zero8
            acc[q, b] = jnp.zeros((box + 2 * SPAN, LANES), F32)
        return 0

    lax.fori_loop(0, n_cubes // 2 * steps, unpack, 0)
    for q in range(n_cubes // 2):
        held[q, box] = jnp.zeros((box + 2 * SPAN, LANES), F32)
        acc[q, box] = jnp.zeros((box + 2 * SPAN, LANES), F32)
    ends = [meta[0, 2, 0]]
    for o in range(1, blocks):
        ends.append(ends[-1] + meta[o, 2, 0])
    active = (ends[-1] - rank + blocks - 1) // blocks

    def slot_of(turn):
        item = rank + blocks * turn
        device, slot = 0, item
        for end in ends[:-1]:
            past = item >= end
            device = device + past.astype(jnp.int32)
            slot = jnp.where(past, item - end, slot)
        return meta[device, 0, slot], meta[device, 1, slot]

    def group(g, _):
        slots = []
        for p in range(2):
            live = (2 * g + p < active).astype(F32)
            first, second = slot_of(jnp.minimum(2 * g + p, active - 1))
            section = second // region_size
            member = second - section * region_size
            ci, cj = id_of(first, 1), id_of(member, section)
            e = [corners[cj, d] - corners[ci, d] for d in range(3)]
            i, j = place_of(first, 1), place_of(member, section)
            slots.append((live, i, j, e))

        def forward(c, _):
            rhos = []
            for t in range(STEP):
                b = c * STEP + t
                us, phis = [], []
                for p, (live, i, j, e) in enumerate(slots):
                    phi = pltpu.roll(held[i // 2, b, SPAN : SPAN + box], HALF * ((p + i) % 2), 1)
                    phis.append(phi * live)
                    bj = b - e[1]
                    at = jnp.where(jnp.logical_and(bj >= 0, bj < box), bj, box)
                    u = held[j // 2, at, pl.ds(SPAN - e[0], box)]
                    amount = lax.rem(e[2] + HALF * (p + j % 2) + LANES, LANES)
                    us.append(pltpu.roll(u, amount, 1))
                u = jnp.where(lane < HALF, us[0], us[1])
                phi = jnp.where(lane < HALF, phis[0], phis[1])
                u_all[b] = u
                phi_all[b] = phi
                rhos.append(u * phi)
            y = lane_transform(lanes_ref[...], jnp.concatenate(rhos, axis=0))
            for t in range(0, STEP, 2):
                pair = row_transform(rows_ref[...], [y[box * t : box * (t + 1)], y[box * (t + 1) : box * (t + 2)]])
                start = pl.multiple_of((c * STEP + t) * box, 8)
                work[pl.ds(start, box)] = pair[0]
                work[pl.ds(start + box, box)] = pair[1]
            return 0

        lax.fori_loop(0, steps, forward, 0)

        def middle(c, _):
            rows = [pl.ds(c * STEP + h, box, stride=box) for h in range(STEP)]
            xs = [work[row] for row in rows]
            ys = []
            for h in range(0, STEP, 2):
                ys.extend(row_transform(rows_ref[...], xs[h : h + 2]))
            ys = [y * green[c * STEP + h] for h, y in enumerate(ys)]
            zs = []
            for h in range(0, STEP, 2):
                zs.extend(row_transform(rows_ref[...], ys[h : h + 2]))
            for row, z in zip(rows, zs):
                turned[row] = z
            return 0

        lax.fori_loop(0, steps, middle, 0)

        def backward(c, _):
            xs = []
            for t in range(0, STEP, 2):
                start = pl.multiple_of((c * STEP + t) * box, 8)
                xs.extend(row_transform(rows_ref[...], [turned[pl.ds(start, box)], turned[pl.ds(start + box, box)]]))
            v_all = lane_transform(lanes_ref[...], jnp.concatenate(xs, axis=0))
            vs = [v_all[box * t : box * (t + 1)] for t in range(STEP)]
            vus = [v * u_all[c * STEP + t] for t, v in enumerate(vs)]
            vps = [v * phi_all[c * STEP + t] for t, v in enumerate(vs)]
            for p, (live, i, j, e) in enumerate(slots):
                half = lane < HALF if p == 0 else lane >= HALF
                near = [(i // 2, c * STEP + t, pl.ds(SPAN, box)) for t in range(STEP)]
                far = []
                for t in range(STEP):
                    bj = c * STEP + t - e[1]
                    at = jnp.where(jnp.logical_and(bj >= 0, bj < box), bj, box)
                    far.append((j // 2, at, pl.ds(SPAN - e[0], box)))
                amount = lax.rem(HALF * (p + j % 2) + LANES - e[2], LANES)
                turns = (HALF * ((p + i) % 2), amount)
                for where, parts, turn in zip((near, far), (vus, vps), turns):
                    adds = [pltpu.roll(jnp.where(half, x, 0.0), turn, 1) for x in parts]
                    olds = [acc[at] for at in where]
                    for at, old, add in zip(where, olds, adds):
                        acc[at] = old + add
            return 0

        lax.fori_loop(0, steps, backward, 0)
        return 0

    lax.fori_loop(0, (active + 1) // 2, group, 0)

    def pack(item, _):
        q, g = item // steps, item % steps
        rows = [acc[q, g * STEP + t, SPAN : SPAN + box] for t in range(STEP)]
        start = pl.multiple_of(g * (box * STEP), LANES)
        for h in range(2):
            for k, block in enumerate(pack_blocks(box, rows, HALF * h, lane)):
                out[2 * q + h, :, pl.ds(start + LANES * k, LANES)] = block.astype(BF16)
        return 0

    lax.fori_loop(0, n_cubes // 2 * steps, pack, 0)


def partners(blocks, regions):
    me, region = lax.axis_index("orb"), lax.axis_index("box")
    up, down = lax.rem(region + 1, regions), lax.rem(region + regions - 1, regions)
    mate = me + 1 - 2 * lax.rem(me, 2)
    peers = [lax.rem(me + 2 * d, blocks) for d in range(1, blocks // 2)]
    mates_peers = [lax.rem(mate + 2 * d, blocks) for d in range(1, blocks // 2)]
    others = [lax.rem(me + d, blocks) for d in range(1, blocks)]
    return me, region, up, down, mate, peers, mates_peers, others


def meet(me, region, up, down, others):
    barrier = pltpu.get_barrier_semaphore()
    devices = [(me, up), (me, down)] + [(o, region) for o in others]
    for device in devices:
        pl.semaphore_signal(barrier, inc=1, device_id=device, device_id_type=pl.DeviceIdType.MESH)
    pl.semaphore_wait(barrier, len(devices))


def remote(src, dst, send, recv, device):
    return pltpu.make_async_remote_copy(
        src_ref=src, dst_ref=dst, send_sem=send, recv_sem=recv, device_id=device,
        device_id_type=pl.DeviceIdType.MESH,
    )


def gather_kernel(dims, mine, meta, out, meta_out, send, recv, meta_send, meta_recv):
    box, own, blocks, regions = dims
    me, region, up, down, mate, peers, mates_peers, others = partners(blocks, regions)
    pieces = box // PIECE
    meet(me, region, up, down, others)
    sent = []

    def piece(o, s, k):
        return out.at[o, pl.ds(s * own, own), pl.ds(PIECE * k, PIECE)]

    def push(src, o, s, k, device):
        copy = remote(src, piece(o, s, k), send.at[len(sent)], recv.at[o, s, k], device)
        copy.start()
        sent.append(copy)

    def arrived(o, s, k):
        ref = piece(o, s, k)
        remote(ref, ref, send.at[0], recv.at[o, s, k], (mate, region)).wait_recv()

    for k in range(pieces):
        src = mine.at[:, pl.ds(PIECE * k, PIECE)]
        push(src, me, 0, k, (me, up))
        push(src, me, 2, k, (me, down))
    metas = []
    for n, o in enumerate(others):
        copy = remote(meta, meta_out.at[me], meta_send.at[n], meta_recv.at[me], (o, region))
        copy.start()
        metas.append(copy)
    for k in range(pieces):
        src = mine.at[:, pl.ds(PIECE * k, PIECE)]
        for peer in peers:
            push(src, me, 1, k, (peer, region))
        push(src, me, 1, k, (mate, region))
    out[me, pl.ds(own, own)] = mine[...]
    meta_out[me] = meta[...]
    for k in range(pieces):
        for s in (0, 2):
            arrived(me, s, k)
            for peer in peers:
                push(piece(me, s, k), me, s, k, (peer, region))
            push(piece(me, s, k), me, s, k, (mate, region))
        for peer in peers:
            arrived(peer, 1, k)
            push(piece(peer, 1, k), peer, 1, k, (mate, region))
    for k in range(pieces):
        for s in (0, 2):
            for peer in peers:
                arrived(peer, s, k)
                push(piece(peer, s, k), peer, s, k, (mate, region))
    for o in [mate] + mates_peers:
        for s in range(3):
            for k in range(pieces):
                arrived(o, s, k)
    for o in others:
        remote(meta, meta_out.at[o], meta_send.at[0], meta_recv.at[o], (mate, region)).wait_recv()
    for copy in sent + metas:
        copy.wait_send()


def reduce_kernel(
    dims, corners, cubes, totals, exchange, gram,
    held, mate_in, peer_out, peer_in, side_out, side_in, mid, columns,
    mate_send, mate_recv, peer_send, peer_recv, side_send, side_recv, col_send, col_recv,
):
    box, own, blocks, regions = dims
    region_size = own * blocks
    me, region, up, down, mate, peers, mates_peers, others = partners(blocks, regions)
    width = box * STEP
    pieces = box // STEP
    lane = lane_ids(box)
    steps = box // STEP
    zero8 = jnp.zeros((SPAN, LANES), F32)
    order = (0, 2, 1)
    meet(me, region, up, down, others)

    def part(ref, o, s, k):
        return ref.at[o, pl.ds(s * own, own), :, pl.ds(width * k, width)]

    def value(ref, o, s, k):
        return ref[o, pl.ds(s * own, own), :, pl.ds(width * k, width)].astype(F32)

    sent = []
    for k in range(pieces):
        for t in mates_peers + [mate]:
            for s in order:
                copy = remote(
                    part(totals, t, s, k), part(mate_in, t // 2, s, k),
                    mate_send.at[t // 2, s, k], mate_recv.at[t // 2, s, k], (mate, region),
                )
                copy.start()
                sent.append(copy)

    def from_mate(t, s, k):
        ref = part(mate_in, t // 2, s, k)
        remote(ref, ref, mate_send.at[0, 0, 0], mate_recv.at[t // 2, s, k], (mate, region)).wait_recv()

    for k in range(pieces):
        for s in order:
            for t in peers:
                from_mate(t, s, k)
                both = value(totals, t, s, k) + value(mate_in, t // 2, s, k)
                peer_out[t // 2, pl.ds(s * own, own), :, pl.ds(width * k, width)] = both.astype(BF16)
                copy = remote(
                    part(peer_out, t // 2, s, k), part(peer_in, me // 2, s, k),
                    peer_send.at[t // 2, s, k], peer_recv.at[me // 2, s, k], (t, region),
                )
                copy.start()
                sent.append(copy)

    def id_of(member):
        return ((member // own) * regions + region) * own + member % own

    def unpack(item, _):
        q, g = item // steps, item % steps
        halves = []
        for h in range(2):
            member = 2 * q + h
            halves.append(load_blocks(box, cubes, (member // own, own + member % own), g))
        for t, row in enumerate(unpack_pair(box, halves[0], halves[1], lane)):
            b = g * STEP + t
            held[q, b, :SPAN] = zero8
            held[q, b, SPAN : SPAN + box] = row
            held[q, b, SPAN + box :] = zero8
        return 0

    lax.fori_loop(0, region_size // 2 * steps, unpack, 0)

    shifts = []
    for col in range(own):
        mine = id_of(me * own + col)
        for k in range(region_size):
            ck = id_of(k)
            shifts.append([corners[ck, d] - corners[mine, d] for d in range(3)])

    def finish(g, sums):
        for side in range(2):
            ref = side_in.at[side, :, :, pl.ds(width * g, width)]
            remote(ref, ref, side_send.at[0, 0], side_recv.at[side, g], (me, up)).wait_recv()
        sums = list(sums)
        for col in range(own):
            blocks_f = [
                a + b + c
                for a, b, c in zip(
                    load_blocks(box, mid, (col,), g),
                    load_blocks(box, side_in, (0, col), g),
                    load_blocks(box, side_in, (1, col), g),
                )
            ]
            for k, block in enumerate(blocks_f):
                exchange[col, :, pl.ds(g * width + LANES * k, LANES)] = block.astype(BF16)
            for t, (x, off) in enumerate(unpack_step(box, blocks_f, lane)):
                b = g * STEP + t
                x = pltpu.roll(x, (-off) % LANES, 1) if off else x
                x = jnp.where(lane < box, x, 0.0)
                for k in range(region_size):
                    n = col * region_size + k
                    e = shifts[n]
                    bj = b - e[1]
                    inside = jnp.logical_and(bj >= 0, bj < box).astype(F32)
                    at = jnp.clip(bj, 0, box - 1)
                    u = held[k // 2, at, pl.ds(SPAN - e[0], box)]
                    amount = lax.rem(e[2] + HALF * (k % 2) + LANES, LANES)
                    product = pltpu.roll(u, amount, 1) * x * inside
                    total = product[:8]
                    for r in range(8, box, 8):
                        total = total + product[r : r + 8]
                    sums[n] = sums[n] + total
        return sums

    sums = [jnp.zeros((8, LANES), F32)] * (own * region_size)
    for k in range(pieces):
        lanes_k = pl.ds(width * k, width)
        for s in order:
            from_mate(me, s, k)
            total = value(totals, me, s, k) + value(mate_in, me // 2, s, k)
            for t in peers:
                ref = part(peer_in, t // 2, s, k)
                remote(ref, ref, peer_send.at[0, 0, 0], peer_recv.at[t // 2, s, k], (t, region)).wait_recv()
                total = total + value(peer_in, t // 2, s, k)
            if s == 1:
                mid[:, :, lanes_k] = total
                continue
            side = s // 2
            side_out[side, :, :, lanes_k] = total.astype(BF16)
            copy = remote(
                side_out.at[side, :, :, lanes_k], side_in.at[side, :, :, lanes_k],
                side_send.at[side, k], side_recv.at[side, k], (me, down if s == 0 else up),
            )
            copy.start()
            sent.append(copy)
        if k > 1:
            sums = finish(k - 2, sums)
    for k in range(pieces - 2, pieces):
        sums = finish(k, sums)

    row8 = lax.broadcasted_iota(jnp.int32, (8, LANES), 0)
    lane8 = lane_ids(8)
    tile = jnp.zeros((8, LANES), F32)
    for col in range(own):
        for k in range(region_size):
            here = jnp.logical_and(row8 == k, lane8 == col)
            tile = jnp.where(here, jnp.sum(sums[col * region_size + k]) * (1.0 / box**3), tile)
    columns[me] = tile
    for n, o in enumerate(others):
        copy = remote(columns.at[me], columns.at[me], col_send.at[n], col_recv.at[me], (o, region))
        copy.start()
        sent.append(copy)
    for o in others:
        remote(columns.at[o], columns.at[o], col_send.at[0], col_recv.at[o], (mate, region)).wait_recv()
    whole = columns[0]
    for o in range(1, blocks):
        whole = whole + pltpu.roll(columns[o], o * own, 1)
    gram[0] = whole[:region_size, :region_size]
    for copy in sent:
        copy.wait_send()


def per_device(orbitals, corners, pairs, counts):
    own, box, plane = orbitals.shape
    blocks = lax.axis_size("orb")
    regions = lax.axis_size("box")
    region_size = own * blocks
    n_cubes = 3 * region_size
    dims = (box, own, blocks, regions)
    slots = pairs.shape[0]
    pieces = box // PIECE
    smem = pl.BlockSpec(memory_space=pltpu.SMEM)
    vmem = pl.BlockSpec(memory_space=pltpu.VMEM)
    dma = pltpu.SemaphoreType.DMA
    meta = jnp.stack([pairs[:, 0], pairs[:, 1], jnp.broadcast_to(counts[:1], (slots,))])
    meta = jnp.pad(meta, ((0, 5), (0, LANES - slots)))
    sends = pieces * (2 + 3 * (blocks - 1))
    gathered, metas = pl.pallas_call(
        functools.partial(gather_kernel, dims),
        out_shape=(
            jax.ShapeDtypeStruct((blocks, 3 * own, box, plane), BF16),
            jax.ShapeDtypeStruct((blocks, 8, LANES), jnp.int32),
        ),
        in_specs=[vmem, vmem],
        out_specs=(vmem, vmem),
        scratch_shapes=[
            dma((sends,)), dma((blocks, 3, pieces)), dma((blocks - 1,)), dma((blocks,)),
        ],
        compiler_params=pltpu.CompilerParams(
            collective_id=0, has_side_effects=True, vmem_limit_bytes=24 * 2**20
        ),
        name="gather_window",
    )(orbitals, meta)
    rows, lanes, green = tables(box)
    padded = (box, box + 2 * SPAN, LANES)
    taller = (box + 1, box + 2 * SPAN, LANES)
    totals = pl.pallas_call(
        functools.partial(pair_kernel, dims),
        out_shape=jax.ShapeDtypeStruct((n_cubes, box, plane), BF16),
        in_specs=[smem, smem, vmem, vmem, vmem, vmem],
        out_specs=vmem,
        scratch_shapes=[
            pltpu.VMEM((n_cubes // 2, *taller), F32),
            pltpu.VMEM((n_cubes // 2, *taller), F32),
            pltpu.VMEM((box * box, LANES), F32),
            pltpu.VMEM((box * box, LANES), F32),
            pltpu.VMEM((box, box, LANES), F32),
            pltpu.VMEM((box, box, LANES), F32),
        ],
        compiler_params=pltpu.CompilerParams(vmem_limit_bytes=60 * 2**20),
        name="pair_potentials",
    )(
        corners, metas, gathered.reshape(n_cubes, box, plane),
        jnp.asarray(rows), jnp.asarray(lanes), jnp.asarray(green),
    )
    chips = blocks // 2
    parts = box // STEP
    wide = (chips, 3 * own, box, plane)
    exchange, gram = pl.pallas_call(
        functools.partial(reduce_kernel, dims),
        out_shape=(
            jax.ShapeDtypeStruct((own, box, plane), BF16),
            jax.ShapeDtypeStruct((1, region_size, region_size), F32),
        ),
        in_specs=[smem, vmem, vmem],
        out_specs=(vmem, vmem),
        scratch_shapes=[
            pltpu.VMEM((region_size // 2, *padded), F32),
            pltpu.VMEM(wide, BF16),
            pltpu.VMEM(wide, BF16),
            pltpu.VMEM(wide, BF16),
            pltpu.VMEM((2, own, box, plane), BF16),
            pltpu.VMEM((2, own, box, plane), BF16),
            pltpu.VMEM((own, box, plane), F32),
            pltpu.VMEM((blocks, 8, LANES), F32),
            dma((chips, 3, parts)), dma((chips, 3, parts)),
            dma((chips, 3, parts)), dma((chips, 3, parts)),
            dma((2, parts)), dma((2, parts)),
            dma((blocks - 1,)), dma((blocks,)),
        ],
        compiler_params=pltpu.CompilerParams(
            collective_id=1, has_side_effects=True, vmem_limit_bytes=48 * 2**20
        ),
        name="reduce_and_gram",
    )(corners, gathered, totals.reshape(blocks, 3 * own, box, plane))
    return exchange, gram


def solution(mesh):
    placed = (P(("orb", "box"), None, None), P(), P(("orb", "box"), None), P(("orb", "box")))
    return jax.shard_map(
        per_device,
        mesh=mesh,
        in_specs=placed,
        out_specs=(P(("orb", "box"), None, None), P("box", None, None)),
        check_vma=False,
    )
```

```python
import functools
import math

import jax
import jax.numpy as jnp
import ml_dtypes
import numpy as np
from jax import lax
from jax.experimental import pallas as pl
from jax.experimental.pallas import tpu as pltpu
from jax.sharding import PartitionSpec as P

SPAN = 8
SCREEN = 0.5
HALF = 64
LANES = 128
STEP = 8
PIECE = 16
F32 = jnp.float32
BF16 = jnp.bfloat16


def tables(box):
    n = np.arange(box)
    angle = (n[:, None] * n[None, :] % box) * (2.0 * math.pi / box)
    cas = np.cos(angle) + np.sin(angle)
    hi = cas.astype(ml_dtypes.bfloat16)
    lo = (cas - hi.astype(np.float64)).astype(ml_dtypes.bfloat16)
    rows = np.concatenate([hi, hi, lo], axis=1)
    lanes = np.zeros((2 * LANES, 2 * LANES), ml_dtypes.bfloat16)
    for p in range(2):
        s = slice(HALF * p, HALF * p + box)
        t = slice(LANES + HALF * p, LANES + HALF * p + box)
        lanes[s, s] = hi
        lanes[t, s] = hi
        lanes[s, t] = lo
    k = np.minimum(n, box - n) * (2.0 * math.pi / box)
    k2 = k * k
    g = -1.0 / (k2[:, None, None] + k2[None, :, None] + k2[None, None, :] + SCREEN) / box**3
    green = np.zeros((box, box, LANES), np.float32)
    for p in range(2):
        green[:, :, HALF * p : HALF * p + box] = g
    return rows, lanes, green


def lane_ids(rows):
    return lax.broadcasted_iota(jnp.int32, (rows, LANES), 1)


def unpack_step(box, blocks, lane):
    out = []
    for t in range(STEP):
        start = box * t
        blk, off = start // LANES, start % LANES
        x = blocks[blk]
        if off + box > LANES:
            x = jnp.where(lane >= off, x, blocks[blk + 1])
        out.append((x, off))
    return out


def unpack_pair(box, first, second, lane):
    out = []
    for (x, off), (y, _) in zip(unpack_step(box, first, lane), unpack_step(box, second, lane)):
        a = pltpu.roll(x, (-off) % LANES, 1) if off else x
        b = pltpu.roll(y, (HALF - off) % LANES, 1) if off != HALF else y
        both = jnp.where(lane < HALF, a, b)
        out.append(jnp.where(lane % HALF < box, both, 0.0))
    return out


def pack_blocks(box, rows, shift, lane):
    n_blocks = box * STEP // LANES
    blocks = [None] * n_blocks
    for t in range(STEP):
        start = box * t
        amount = (start - shift) % LANES
        x = pltpu.roll(rows[t], amount, 1) if amount else rows[t]
        for blk in range(start // LANES, (start + box - 1) // LANES + 1):
            lo = start - blk * LANES
            if blocks[blk] is None:
                blocks[blk] = x
            else:
                blocks[blk] = jnp.where(lane >= max(lo, 0), x, blocks[blk])
    return blocks


def load_blocks(box, ref, lead, g):
    width = box * STEP
    start = pl.multiple_of(g * width, LANES)
    return [
        ref[(*lead, slice(None), pl.ds(start + LANES * k, LANES))].astype(F32)
        for k in range(width // LANES)
    ]


def split_rows(x):
    hi = x.astype(BF16)
    lo = (x - hi.astype(F32)).astype(BF16)
    return hi, lo


def row_transform(t_rows, xs):
    x = jnp.concatenate(xs, axis=1)
    hi, lo = split_rows(x)
    stacked = jnp.concatenate([hi, lo, hi], axis=0)
    y = jnp.dot(t_rows, stacked, preferred_element_type=F32)
    return y[:, :LANES], y[:, LANES:]


def lane_transform(t_lanes, x):
    hi, lo = split_rows(x)
    y = jnp.dot(jnp.concatenate([hi, lo], axis=1), t_lanes, preferred_element_type=F32)
    return y[:, :LANES] + y[:, LANES:]


def pair_kernel(
    dims, corners, meta, cubes, rows_ref, lanes_ref, green, out, held, acc, work, turned, u_all, phi_all
):
    box, own, blocks, regions = dims
    region_size = own * blocks
    n_cubes = 3 * region_size
    box_index, rank = lax.axis_index("box"), lax.axis_index("orb")
    lane = lane_ids(box)
    steps = box // STEP
    zero8 = jnp.zeros((SPAN, LANES), F32)

    def place_of(member, section):
        return (member // own) * (3 * own) + section * own + member % own

    def id_of(member, section):
        neighbour = lax.rem(box_index + section - 1 + regions, regions)
        return ((member // own) * regions + neighbour) * own + member % own

    def unpack(item, _):
        q, g = item // steps, item % steps
        first = load_blocks(box, cubes, (2 * q,), g)
        second = load_blocks(box, cubes, (2 * q + 1,), g)
        for t, row in enumerate(unpack_pair(box, first, second, lane)):
            b = g * STEP + t
            held[q, b, :SPAN] = zero8
            held[q, b, SPAN : SPAN + box] = row
            held[q, b, SPAN + box :] = zero8
            acc[q, b] = jnp.zeros((box + 2 * SPAN, LANES), F32)
        return 0

    lax.fori_loop(0, n_cubes // 2 * steps, unpack, 0)
    for q in range(n_cubes // 2):
        held[q, box] = jnp.zeros((box + 2 * SPAN, LANES), F32)
        acc[q, box] = jnp.zeros((box + 2 * SPAN, LANES), F32)
    ends = [meta[0, 2, 0]]
    for o in range(1, blocks):
        ends.append(ends[-1] + meta[o, 2, 0])
    active = (ends[-1] - rank + blocks - 1) // blocks

    def slot_of(turn):
        item = rank + blocks * turn
        device, slot = 0, item
        for end in ends[:-1]:
            past = item >= end
            device = device + past.astype(jnp.int32)
            slot = jnp.where(past, item - end, slot)
        return meta[device, 0, slot], meta[device, 1, slot]

    def group(g, _):
        slots = []
        for p in range(2):
            live = (2 * g + p < active).astype(F32)
            first, second = slot_of(jnp.minimum(2 * g + p, active - 1))
            section = second // region_size
            member = second - section * region_size
            ci, cj = id_of(first, 1), id_of(member, section)
            e = [corners[cj, d] - corners[ci, d] for d in range(3)]
            i, j = place_of(first, 1), place_of(member, section)
            slots.append((live, i, j, e))

        (live_0, i_0, j_0, e_0), (live_1, i_1, j_1, e_1) = slots
        row_id = lax.broadcasted_iota(jnp.int32, (2 * LANES, LANES), 0)
        lane_id = lane_ids(2 * LANES)
        cell = lane_id % HALF
        low = lane_id < HALF
        here = cell < box
        live = jnp.where(low, live_0, live_1)
        source = jnp.where(low, HALF * (i_0 % 2), LANES + HALF * (i_1 % 2)) + cell
        take_i = jnp.where(jnp.logical_and(row_id == source, here), live, 0.0).astype(BF16)
        moved = cell - jnp.where(low, e_0[2], e_1[2])
        source = jnp.where(low, HALF * (j_0 % 2), LANES + HALF * (j_1 % 2)) + moved
        fits = jnp.logical_and(here, jnp.logical_and(moved >= 0, moved < box))
        take_j = jnp.where(jnp.logical_and(row_id == source, fits), 1.0, 0.0).astype(BF16)

        def give(position, step, p):
            moved = cell + step
            fits = jnp.logical_and(here, jnp.logical_and(moved >= 0, moved < box))
            fits = jnp.logical_and(fits, lane_id // HALF == position % 2)
            return jnp.where(jnp.logical_and(row_id % LANES == HALF * p + moved, fits), 1.0, 0.0)

        give_i = jnp.concatenate([give(i_0, 0, 0), give(i_1, 0, 1)], axis=1).astype(BF16)
        give_j = jnp.concatenate([give(j_0, e_0[2], 0), give(j_1, e_1[2], 1)], axis=1).astype(BF16)

        def far_row(b, e):
            bj = b - e[1]
            return jnp.where(jnp.logical_and(bj >= 0, bj < box), bj, box)

        def forward(c, _):
            firsts, seconds = [], []
            for t in range(STEP):
                b = c * STEP + t
                firsts.append(jnp.concatenate([held[i // 2, b, SPAN : SPAN + box] for _, i, _, _ in slots], axis=1))
                seconds.append(
                    jnp.concatenate(
                        [held[j // 2, far_row(b, e), pl.ds(SPAN - e[0], box)] for _, _, j, e in slots], axis=1
                    )
                )
            phi = jnp.dot(jnp.concatenate(firsts, axis=0).astype(BF16), take_i, preferred_element_type=F32)
            u = jnp.dot(jnp.concatenate(seconds, axis=0).astype(BF16), take_j, preferred_element_type=F32)
            for t in range(STEP):
                u_all[c * STEP + t] = u[box * t : box * (t + 1)]
                phi_all[c * STEP + t] = phi[box * t : box * (t + 1)]
            rhos = [u * phi]
            y = lane_transform(lanes_ref[...], jnp.concatenate(rhos, axis=0))
            for t in range(0, STEP, 2):
                pair = row_transform(rows_ref[...], [y[box * t : box * (t + 1)], y[box * (t + 1) : box * (t + 2)]])
                start = pl.multiple_of((c * STEP + t) * box, 8)
                work[pl.ds(start, box)] = pair[0]
                work[pl.ds(start + box, box)] = pair[1]
            return 0

        lax.fori_loop(0, steps, forward, 0)

        def middle(c, _):
            rows = [pl.ds(c * STEP + h, box, stride=box) for h in range(STEP)]
            xs = [work[row] for row in rows]
            ys = []
            for h in range(0, STEP, 2):
                ys.extend(row_transform(rows_ref[...], xs[h : h + 2]))
            ys = [y * green[c * STEP + h] for h, y in enumerate(ys)]
            zs = []
            for h in range(0, STEP, 2):
                zs.extend(row_transform(rows_ref[...], ys[h : h + 2]))
            for row, z in zip(rows, zs):
                turned[row] = z
            return 0

        lax.fori_loop(0, steps, middle, 0)

        def backward(c, _):
            xs = []
            for t in range(0, STEP, 2):
                start = pl.multiple_of((c * STEP + t) * box, 8)
                xs.extend(row_transform(rows_ref[...], [turned[pl.ds(start, box)], turned[pl.ds(start + box, box)]]))
            v_all = lane_transform(lanes_ref[...], jnp.concatenate(xs, axis=0))
            u = jnp.concatenate([u_all[c * STEP + t] for t in range(STEP)], axis=0)
            phi = jnp.concatenate([phi_all[c * STEP + t] for t in range(STEP)], axis=0)
            vu = jnp.dot(jnp.concatenate(split_rows(v_all * u), axis=1), give_i, preferred_element_type=F32)
            vp = jnp.dot(jnp.concatenate(split_rows(v_all * phi), axis=1), give_j, preferred_element_type=F32)
            for p, (_, i, j, e) in enumerate(slots):
                near = [(i // 2, c * STEP + t, pl.ds(SPAN, box)) for t in range(STEP)]
                far = [(j // 2, far_row(c * STEP + t, e), pl.ds(SPAN - e[0], box)) for t in range(STEP)]
                for where, values in ((near, vu), (far, vp)):
                    olds = [acc[at] for at in where]
                    for t, (at, old) in enumerate(zip(where, olds)):
                        acc[at] = old + values[box * t : box * (t + 1), LANES * p : LANES * (p + 1)]
            return 0

        lax.fori_loop(0, steps, backward, 0)
        return 0

    lax.fori_loop(0, (active + 1) // 2, group, 0)

    def pack(item, _):
        q, g = item // steps, item % steps
        rows = [acc[q, g * STEP + t, SPAN : SPAN + box] for t in range(STEP)]
        start = pl.multiple_of(g * (box * STEP), LANES)
        for h in range(2):
            for k, block in enumerate(pack_blocks(box, rows, HALF * h, lane)):
                out[2 * q + h, :, pl.ds(start + LANES * k, LANES)] = block.astype(BF16)
        return 0

    lax.fori_loop(0, n_cubes // 2 * steps, pack, 0)


def partners(blocks, regions):
    me, region = lax.axis_index("orb"), lax.axis_index("box")
    up, down = lax.rem(region + 1, regions), lax.rem(region + regions - 1, regions)
    mate = me + 1 - 2 * lax.rem(me, 2)
    peers = [lax.rem(me + 2 * d, blocks) for d in range(1, blocks // 2)]
    mates_peers = [lax.rem(mate + 2 * d, blocks) for d in range(1, blocks // 2)]
    others = [lax.rem(me + d, blocks) for d in range(1, blocks)]
    return me, region, up, down, mate, peers, mates_peers, others


def meet(me, region, up, down, others):
    barrier = pltpu.get_barrier_semaphore()
    devices = [(me, up), (me, down)] + [(o, region) for o in others]
    for device in devices:
        pl.semaphore_signal(barrier, inc=1, device_id=device, device_id_type=pl.DeviceIdType.MESH)
    pl.semaphore_wait(barrier, len(devices))


def remote(src, dst, send, recv, device):
    return pltpu.make_async_remote_copy(
        src_ref=src, dst_ref=dst, send_sem=send, recv_sem=recv, device_id=device,
        device_id_type=pl.DeviceIdType.MESH,
    )


def gather_kernel(dims, mine, meta, out, meta_out, send, recv, meta_send, meta_recv):
    box, own, blocks, regions = dims
    me, region, up, down, mate, peers, mates_peers, others = partners(blocks, regions)
    pieces = box // PIECE
    meet(me, region, up, down, others)
    sent = []

    def piece(o, s, k):
        return out.at[o, pl.ds(s * own, own), pl.ds(PIECE * k, PIECE)]

    def push(src, o, s, k, device):
        copy = remote(src, piece(o, s, k), send.at[len(sent)], recv.at[o, s, k], device)
        copy.start()
        sent.append(copy)

    def arrived(o, s, k):
        ref = piece(o, s, k)
        remote(ref, ref, send.at[0], recv.at[o, s, k], (mate, region)).wait_recv()

    for k in range(pieces):
        src = mine.at[:, pl.ds(PIECE * k, PIECE)]
        push(src, me, 0, k, (me, up))
        push(src, me, 2, k, (me, down))
    metas = []
    for n, o in enumerate(others):
        copy = remote(meta, meta_out.at[me], meta_send.at[n], meta_recv.at[me], (o, region))
        copy.start()
        metas.append(copy)
    for k in range(pieces):
        src = mine.at[:, pl.ds(PIECE * k, PIECE)]
        for peer in peers:
            push(src, me, 1, k, (peer, region))
        push(src, me, 1, k, (mate, region))
    out[me, pl.ds(own, own)] = mine[...]
    meta_out[me] = meta[...]
    for k in range(pieces):
        for s in (0, 2):
            arrived(me, s, k)
            for peer in peers:
                push(piece(me, s, k), me, s, k, (peer, region))
            push(piece(me, s, k), me, s, k, (mate, region))
        for peer in peers:
            arrived(peer, 1, k)
            push(piece(peer, 1, k), peer, 1, k, (mate, region))
    for k in range(pieces):
        for s in (0, 2):
            for peer in peers:
                arrived(peer, s, k)
                push(piece(peer, s, k), peer, s, k, (mate, region))
    for o in [mate] + mates_peers:
        for s in range(3):
            for k in range(pieces):
                arrived(o, s, k)
    for o in others:
        remote(meta, meta_out.at[o], meta_send.at[0], meta_recv.at[o], (mate, region)).wait_recv()
    for copy in sent + metas:
        copy.wait_send()


def reduce_kernel(
    dims, corners, cubes, totals, exchange, gram,
    held, mate_in, peer_out, peer_in, side_out, side_in, mid, columns,
    mate_send, mate_recv, peer_send, peer_recv, side_send, side_recv, col_send, col_recv,
):
    box, own, blocks, regions = dims
    region_size = own * blocks
    me, region, up, down, mate, peers, mates_peers, others = partners(blocks, regions)
    pieces = box // PIECE
    lane = lane_ids(box)
    steps = box // STEP
    zero8 = jnp.zeros((SPAN, LANES), F32)
    order = (0, 2, 1)
    meet(me, region, up, down, others)

    def part(ref, o, s, k):
        return ref.at[o, pl.ds(s * own, own), pl.ds(PIECE * k, PIECE)]

    def value(ref, o, s, k):
        return ref[o, pl.ds(s * own, own), pl.ds(PIECE * k, PIECE)].astype(F32)

    sent = []
    for t in mates_peers + [mate]:
        for s in order:
            for k in range(pieces):
                copy = remote(
                    part(totals, t, s, k), part(mate_in, t // 2, s, k),
                    mate_send.at[t // 2, s, k], mate_recv.at[t // 2, s, k], (mate, region),
                )
                copy.start()
                sent.append(copy)

    def from_mate(t, s, k):
        ref = part(mate_in, t // 2, s, k)
        remote(ref, ref, mate_send.at[0, 0, 0], mate_recv.at[t // 2, s, k], (mate, region)).wait_recv()

    for s in order:
        for k in range(pieces):
            for t in peers:
                from_mate(t, s, k)
                both = value(totals, t, s, k) + value(mate_in, t // 2, s, k)
                peer_out[t // 2, pl.ds(s * own, own), pl.ds(PIECE * k, PIECE)] = both.astype(BF16)
                copy = remote(
                    part(peer_out, t // 2, s, k), part(peer_in, me // 2, s, k),
                    peer_send.at[t // 2, s, k], peer_recv.at[me // 2, s, k], (t, region),
                )
                copy.start()
                sent.append(copy)

    def id_of(member):
        return ((member // own) * regions + region) * own + member % own

    def unpack(item, _):
        q, g = item // steps, item % steps
        halves = []
        for h in range(2):
            member = 2 * q + h
            halves.append(load_blocks(box, cubes, (member // own, own + member % own), g))
        for t, row in enumerate(unpack_pair(box, halves[0], halves[1], lane)):
            b = g * STEP + t
            held[q, b, :SPAN] = zero8
            held[q, b, SPAN : SPAN + box] = row
            held[q, b, SPAN + box :] = zero8
        return 0

    lax.fori_loop(0, region_size // 2 * steps, unpack, 0)

    for s in order:
        for k in range(pieces):
            from_mate(me, s, k)
            total = value(totals, me, s, k) + value(mate_in, me // 2, s, k)
            for t in peers:
                ref = part(peer_in, t // 2, s, k)
                remote(ref, ref, peer_send.at[0, 0, 0], peer_recv.at[t // 2, s, k], (t, region)).wait_recv()
                total = total + value(peer_in, t // 2, s, k)
            if s == 1:
                mid[:, pl.ds(PIECE * k, PIECE)] = total
                continue
            side = s // 2
            side_out[side, :, pl.ds(PIECE * k, PIECE)] = total.astype(BF16)
            copy = remote(
                side_out.at[side, :, pl.ds(PIECE * k, PIECE)], side_in.at[side, :, pl.ds(PIECE * k, PIECE)],
                side_send.at[side, k], side_recv.at[side, k], (me, down if s == 0 else up),
            )
            copy.start()
            sent.append(copy)
    for k in range(pieces):
        for side in range(2):
            ref = side_in.at[side, :, pl.ds(PIECE * k, PIECE)]
            remote(ref, ref, side_send.at[0, 0], side_recv.at[side, k], (me, up)).wait_recv()

    row8 = lax.broadcasted_iota(jnp.int32, (8, LANES), 0)
    lane8 = lane_ids(8)
    tile = jnp.zeros((8, LANES), F32)
    for col in range(own):
        mine = id_of(me * own + col)
        shifts = []
        for k in range(region_size):
            ck = id_of(k)
            shifts.append([corners[ck, d] - corners[mine, d] for d in range(3)])

        def step(g, sums):
            blocks_f = [
                a + b + c
                for a, b, c in zip(
                    load_blocks(box, mid, (col,), g),
                    load_blocks(box, side_in, (0, col), g),
                    load_blocks(box, side_in, (1, col), g),
                )
            ]
            start = pl.multiple_of(g * (box * STEP), LANES)
            for k, block in enumerate(blocks_f):
                exchange[col, :, pl.ds(start + LANES * k, LANES)] = block.astype(BF16)
            sums = list(sums)
            for t, (x, off) in enumerate(unpack_step(box, blocks_f, lane)):
                b = g * STEP + t
                x = pltpu.roll(x, (-off) % LANES, 1) if off else x
                x = jnp.where(lane < box, x, 0.0)
                for k in range(region_size):
                    e = shifts[k]
                    bj = b - e[1]
                    inside = jnp.logical_and(bj >= 0, bj < box).astype(F32)
                    at = jnp.clip(bj, 0, box - 1)
                    u = held[k // 2, at, pl.ds(SPAN - e[0], box)]
                    amount = lax.rem(e[2] + HALF * (k % 2) + LANES, LANES)
                    product = pltpu.roll(u, amount, 1) * x * inside
                    total = product[:8]
                    for r in range(8, box, 8):
                        total = total + product[r : r + 8]
                    sums[k] = sums[k] + total
            return tuple(sums)

        sums = lax.fori_loop(0, steps, step, tuple(jnp.zeros((8, LANES), F32) for _ in range(region_size)))
        for k in range(region_size):
            here = jnp.logical_and(row8 == k, lane8 == col)
            tile = jnp.where(here, jnp.sum(sums[k]) * (1.0 / box**3), tile)
    columns[me] = tile
    for n, o in enumerate(others):
        copy = remote(columns.at[me], columns.at[me], col_send.at[n], col_recv.at[me], (o, region))
        copy.start()
        sent.append(copy)
    for o in others:
        remote(columns.at[o], columns.at[o], col_send.at[0], col_recv.at[o], (mate, region)).wait_recv()
    whole = columns[0]
    for o in range(1, blocks):
        whole = whole + pltpu.roll(columns[o], o * own, 1)
    gram[0] = whole[:region_size, :region_size]
    for copy in sent:
        copy.wait_send()


def per_device(orbitals, corners, pairs, counts):
    own, box, plane = orbitals.shape
    blocks = lax.axis_size("orb")
    regions = lax.axis_size("box")
    region_size = own * blocks
    n_cubes = 3 * region_size
    dims = (box, own, blocks, regions)
    slots = pairs.shape[0]
    pieces = box // PIECE
    smem = pl.BlockSpec(memory_space=pltpu.SMEM)
    vmem = pl.BlockSpec(memory_space=pltpu.VMEM)
    dma = pltpu.SemaphoreType.DMA
    meta = jnp.stack([pairs[:, 0], pairs[:, 1], jnp.broadcast_to(counts[:1], (slots,))])
    meta = jnp.pad(meta, ((0, 5), (0, LANES - slots)))
    sends = pieces * (2 + 3 * (blocks - 1))
    gathered, metas = pl.pallas_call(
        functools.partial(gather_kernel, dims),
        out_shape=(
            jax.ShapeDtypeStruct((blocks, 3 * own, box, plane), BF16),
            jax.ShapeDtypeStruct((blocks, 8, LANES), jnp.int32),
        ),
        in_specs=[vmem, vmem],
        out_specs=(vmem, vmem),
        scratch_shapes=[
            dma((sends,)), dma((blocks, 3, pieces)), dma((blocks - 1,)), dma((blocks,)),
        ],
        compiler_params=pltpu.CompilerParams(
            collective_id=0, has_side_effects=True, vmem_limit_bytes=24 * 2**20
        ),
        name="gather_window",
    )(orbitals, meta)
    rows, lanes, green = tables(box)
    padded = (box, box + 2 * SPAN, LANES)
    taller = (box + 1, box + 2 * SPAN, LANES)
    totals = pl.pallas_call(
        functools.partial(pair_kernel, dims),
        out_shape=jax.ShapeDtypeStruct((n_cubes, box, plane), BF16),
        in_specs=[smem, smem, vmem, vmem, vmem, vmem],
        out_specs=vmem,
        scratch_shapes=[
            pltpu.VMEM((n_cubes // 2, *taller), F32),
            pltpu.VMEM((n_cubes // 2, *taller), F32),
            pltpu.VMEM((box * box, LANES), F32),
            pltpu.VMEM((box * box, LANES), F32),
            pltpu.VMEM((box, box, LANES), F32),
            pltpu.VMEM((box, box, LANES), F32),
        ],
        compiler_params=pltpu.CompilerParams(vmem_limit_bytes=60 * 2**20),
        name="pair_potentials",
    )(
        corners, metas, gathered.reshape(n_cubes, box, plane),
        jnp.asarray(rows), jnp.asarray(lanes), jnp.asarray(green),
    )
    chips = blocks // 2
    wide = (chips, 3 * own, box, plane)
    exchange, gram = pl.pallas_call(
        functools.partial(reduce_kernel, dims),
        out_shape=(
            jax.ShapeDtypeStruct((own, box, plane), BF16),
            jax.ShapeDtypeStruct((1, region_size, region_size), F32),
        ),
        in_specs=[smem, vmem, vmem],
        out_specs=(vmem, vmem),
        scratch_shapes=[
            pltpu.VMEM((region_size // 2, *padded), F32),
            pltpu.VMEM(wide, BF16),
            pltpu.VMEM(wide, BF16),
            pltpu.VMEM(wide, BF16),
            pltpu.VMEM((2, own, box, plane), BF16),
            pltpu.VMEM((2, own, box, plane), BF16),
            pltpu.VMEM((own, box, plane), F32),
            pltpu.VMEM((blocks, 8, LANES), F32),
            dma((chips, 3, pieces)), dma((chips, 3, pieces)),
            dma((chips, 3, pieces)), dma((chips, 3, pieces)),
            dma((2, pieces)), dma((2, pieces)),
            dma((blocks - 1,)), dma((blocks,)),
        ],
        compiler_params=pltpu.CompilerParams(
            collective_id=1, has_side_effects=True, vmem_limit_bytes=48 * 2**20
        ),
        name="reduce_and_gram",
    )(corners, gathered, totals.reshape(blocks, 3 * own, box, plane))
    return exchange, gram


def solution(mesh):
    placed = (P(("orb", "box"), None, None), P(), P(("orb", "box"), None), P(("orb", "box")))
    return jax.shard_map(
        per_device,
        mesh=mesh,
        in_specs=placed,
        out_specs=(P(("orb", "box"), None, None), P("box", None, None)),
        check_vma=False,
    )
```

```python
import functools
import math

import jax
import jax.numpy as jnp
import ml_dtypes
import numpy as np
from jax import lax
from jax.experimental import pallas as pl
from jax.experimental.pallas import tpu as pltpu
from jax.sharding import PartitionSpec as P

SPAN = 8
SCREEN = 0.5
HALF = 64
LANES = 128
STEP = 8
PIECE = 16
F32 = jnp.float32
BF16 = jnp.bfloat16


def tables(box):
    n = np.arange(box)
    angle = (n[:, None] * n[None, :] % box) * (2.0 * math.pi / box)
    cas = np.cos(angle) + np.sin(angle)
    hi = cas.astype(ml_dtypes.bfloat16)
    lo = (cas - hi.astype(np.float64)).astype(ml_dtypes.bfloat16)
    rows = np.concatenate([hi, hi, lo], axis=1)
    lanes = np.zeros((2 * LANES, 2 * LANES), ml_dtypes.bfloat16)
    for p in range(2):
        s = slice(HALF * p, HALF * p + box)
        t = slice(LANES + HALF * p, LANES + HALF * p + box)
        lanes[s, s] = hi
        lanes[t, s] = hi
        lanes[s, t] = lo
    k = np.minimum(n, box - n) * (2.0 * math.pi / box)
    k2 = k * k
    g = -1.0 / (k2[:, None, None] + k2[None, :, None] + k2[None, None, :] + SCREEN) / box**3
    green = np.zeros((box, box, LANES), np.float32)
    for p in range(2):
        green[:, :, HALF * p : HALF * p + box] = g
    return rows, lanes, green


def lane_ids(rows):
    return lax.broadcasted_iota(jnp.int32, (rows, LANES), 1)


def unpack_step(box, blocks, lane):
    out = []
    for t in range(STEP):
        start = box * t
        blk, off = start // LANES, start % LANES
        x = blocks[blk]
        if off + box > LANES:
            x = jnp.where(lane >= off, x, blocks[blk + 1])
        out.append((x, off))
    return out


def unpack_pair(box, first, second, lane):
    out = []
    for (x, off), (y, _) in zip(unpack_step(box, first, lane), unpack_step(box, second, lane)):
        a = pltpu.roll(x, (-off) % LANES, 1) if off else x
        b = pltpu.roll(y, (HALF - off) % LANES, 1) if off != HALF else y
        both = jnp.where(lane < HALF, a, b)
        out.append(jnp.where(lane % HALF < box, both, 0.0))
    return out


def pack_blocks(box, rows, shift, lane):
    n_blocks = box * STEP // LANES
    blocks = [None] * n_blocks
    for t in range(STEP):
        start = box * t
        amount = (start - shift) % LANES
        x = pltpu.roll(rows[t], amount, 1) if amount else rows[t]
        for blk in range(start // LANES, (start + box - 1) // LANES + 1):
            lo = start - blk * LANES
            if blocks[blk] is None:
                blocks[blk] = x
            else:
                blocks[blk] = jnp.where(lane >= max(lo, 0), x, blocks[blk])
    return blocks


def load_blocks(box, ref, lead, g):
    width = box * STEP
    start = pl.multiple_of(g * width, LANES)
    return [
        ref[(*lead, slice(None), pl.ds(start + LANES * k, LANES))].astype(F32)
        for k in range(width // LANES)
    ]


def split_rows(x):
    hi = x.astype(BF16)
    lo = (x - hi.astype(F32)).astype(BF16)
    return hi, lo


def row_transform(t_rows, xs):
    x = jnp.concatenate(xs, axis=1)
    hi, lo = split_rows(x)
    stacked = jnp.concatenate([hi, lo, hi], axis=0)
    y = jnp.dot(t_rows, stacked, preferred_element_type=F32)
    return y[:, :LANES], y[:, LANES:]


def lane_transform(t_lanes, x):
    hi, lo = split_rows(x)
    y = jnp.dot(jnp.concatenate([hi, lo], axis=1), t_lanes, preferred_element_type=F32)
    return y[:, :LANES] + y[:, LANES:]


def pair_kernel(
    dims, corners, meta, cubes, rows_ref, lanes_ref, green, out, held, acc, work, turned, u_all, phi_all
):
    box, own, blocks, regions = dims
    region_size = own * blocks
    n_cubes = 3 * region_size
    box_index, rank = lax.axis_index("box"), lax.axis_index("orb")
    lane = lane_ids(box)
    steps = box // STEP
    zero8 = jnp.zeros((SPAN, LANES), F32)

    def place_of(member, section):
        return (member // own) * (3 * own) + section * own + member % own

    def id_of(member, section):
        neighbour = lax.rem(box_index + section - 1 + regions, regions)
        return ((member // own) * regions + neighbour) * own + member % own

    def unpack(item, _):
        q, g = item // steps, item % steps
        first = load_blocks(box, cubes, (2 * q,), g)
        second = load_blocks(box, cubes, (2 * q + 1,), g)
        for t, row in enumerate(unpack_pair(box, first, second, lane)):
            b = g * STEP + t
            held[q, b, :SPAN] = zero8
            held[q, b, SPAN : SPAN + box] = row
            held[q, b, SPAN + box :] = zero8
            acc[q, b] = jnp.zeros((box + 2 * SPAN, LANES), F32)
        return 0

    lax.fori_loop(0, n_cubes // 2 * steps, unpack, 0)
    for q in range(n_cubes // 2):
        held[q, box] = jnp.zeros((box + 2 * SPAN, LANES), F32)
        acc[q, box] = jnp.zeros((box + 2 * SPAN, LANES), F32)
    ends = [meta[0, 2, 0]]
    for o in range(1, blocks):
        ends.append(ends[-1] + meta[o, 2, 0])
    active = (ends[-1] - rank + blocks - 1) // blocks

    def slot_of(turn):
        item = rank + blocks * turn
        device, slot = 0, item
        for end in ends[:-1]:
            past = item >= end
            device = device + past.astype(jnp.int32)
            slot = jnp.where(past, item - end, slot)
        return meta[device, 0, slot], meta[device, 1, slot]

    def group(g, _):
        slots = []
        for p in range(2):
            live = (2 * g + p < active).astype(F32)
            first, second = slot_of(jnp.minimum(2 * g + p, active - 1))
            section = second // region_size
            member = second - section * region_size
            ci, cj = id_of(first, 1), id_of(member, section)
            e = [corners[cj, d] - corners[ci, d] for d in range(3)]
            i, j = place_of(first, 1), place_of(member, section)
            slots.append((live, i, j, e))

        (live_0, i_0, j_0, e_0), (live_1, i_1, j_1, e_1) = slots
        row_id = lax.broadcasted_iota(jnp.int32, (2 * LANES, LANES), 0)
        lane_id = lane_ids(2 * LANES)
        cell = lane_id % HALF
        low = lane_id < HALF
        here = cell < box
        live = jnp.where(low, live_0, live_1)
        source = jnp.where(low, HALF * (i_0 % 2), LANES + HALF * (i_1 % 2)) + cell
        take_i = jnp.where(jnp.logical_and(row_id == source, here), live, 0.0).astype(BF16)
        moved = cell - jnp.where(low, e_0[2], e_1[2])
        source = jnp.where(low, HALF * (j_0 % 2), LANES + HALF * (j_1 % 2)) + moved
        fits = jnp.logical_and(here, jnp.logical_and(moved >= 0, moved < box))
        take_j = jnp.where(jnp.logical_and(row_id == source, fits), 1.0, 0.0).astype(BF16)

        def give(position, step, p):
            moved = cell + step
            fits = jnp.logical_and(here, jnp.logical_and(moved >= 0, moved < box))
            fits = jnp.logical_and(fits, lane_id // HALF == position % 2)
            return jnp.where(jnp.logical_and(row_id % LANES == HALF * p + moved, fits), 1.0, 0.0)

        give_i = jnp.concatenate([give(i_0, 0, 0), give(i_1, 0, 1)], axis=1).astype(BF16)
        give_j = jnp.concatenate([give(j_0, e_0[2], 0), give(j_1, e_1[2], 1)], axis=1).astype(BF16)

        def far_row(b, e):
            bj = b - e[1]
            return jnp.where(jnp.logical_and(bj >= 0, bj < box), bj, box)

        def forward(c, _):
            firsts, seconds = [], []
            for t in range(STEP):
                b = c * STEP + t
                firsts.append(jnp.concatenate([held[i // 2, b, SPAN : SPAN + box] for _, i, _, _ in slots], axis=1))
                seconds.append(
                    jnp.concatenate(
                        [held[j // 2, far_row(b, e), pl.ds(SPAN - e[0], box)] for _, _, j, e in slots], axis=1
                    )
                )
            phi = jnp.dot(jnp.concatenate(firsts, axis=0).astype(BF16), take_i, preferred_element_type=F32)
            u = jnp.dot(jnp.concatenate(seconds, axis=0).astype(BF16), take_j, preferred_element_type=F32)
            for t in range(STEP):
                u_all[c * STEP + t] = u[box * t : box * (t + 1)]
                phi_all[c * STEP + t] = phi[box * t : box * (t + 1)]
            rhos = [u * phi]
            y = lane_transform(lanes_ref[...], jnp.concatenate(rhos, axis=0))
            for t in range(0, STEP, 2):
                pair = row_transform(rows_ref[...], [y[box * t : box * (t + 1)], y[box * (t + 1) : box * (t + 2)]])
                start = pl.multiple_of((c * STEP + t) * box, 8)
                work[pl.ds(start, box)] = pair[0]
                work[pl.ds(start + box, box)] = pair[1]
            return 0

        lax.fori_loop(0, steps, forward, 0, unroll=2)

        def middle(c, _):
            rows = [pl.ds(c * STEP + h, box, stride=box) for h in range(STEP)]
            xs = [work[row] for row in rows]
            ys = []
            for h in range(0, STEP, 2):
                ys.extend(row_transform(rows_ref[...], xs[h : h + 2]))
            ys = [y * green[c * STEP + h] for h, y in enumerate(ys)]
            zs = []
            for h in range(0, STEP, 2):
                zs.extend(row_transform(rows_ref[...], ys[h : h + 2]))
            for row, z in zip(rows, zs):
                turned[row] = z
            return 0

        lax.fori_loop(0, steps, middle, 0, unroll=2)

        def backward(c, _):
            xs = []
            for t in range(0, STEP, 2):
                start = pl.multiple_of((c * STEP + t) * box, 8)
                xs.extend(row_transform(rows_ref[...], [turned[pl.ds(start, box)], turned[pl.ds(start + box, box)]]))
            v_all = lane_transform(lanes_ref[...], jnp.concatenate(xs, axis=0))
            u = jnp.concatenate([u_all[c * STEP + t] for t in range(STEP)], axis=0)
            phi = jnp.concatenate([phi_all[c * STEP + t] for t in range(STEP)], axis=0)
            vu = jnp.dot(jnp.concatenate(split_rows(v_all * u), axis=1), give_i, preferred_element_type=F32)
            vp = jnp.dot(jnp.concatenate(split_rows(v_all * phi), axis=1), give_j, preferred_element_type=F32)
            for p, (_, i, j, e) in enumerate(slots):
                near = [(i // 2, c * STEP + t, pl.ds(SPAN, box)) for t in range(STEP)]
                far = [(j // 2, far_row(c * STEP + t, e), pl.ds(SPAN - e[0], box)) for t in range(STEP)]
                for where, values in ((near, vu), (far, vp)):
                    olds = [acc[at] for at in where]
                    for t, (at, old) in enumerate(zip(where, olds)):
                        acc[at] = old + values[box * t : box * (t + 1), LANES * p : LANES * (p + 1)]
            return 0

        lax.fori_loop(0, steps, backward, 0, unroll=2)
        return 0

    lax.fori_loop(0, (active + 1) // 2, group, 0)

    def pack(item, _):
        q, g = item // steps, item % steps
        rows = [acc[q, g * STEP + t, SPAN : SPAN + box] for t in range(STEP)]
        start = pl.multiple_of(g * (box * STEP), LANES)
        for h in range(2):
            for k, block in enumerate(pack_blocks(box, rows, HALF * h, lane)):
                out[2 * q + h, :, pl.ds(start + LANES * k, LANES)] = block.astype(BF16)
        return 0

    lax.fori_loop(0, n_cubes // 2 * steps, pack, 0)


def partners(blocks, regions):
    me, region = lax.axis_index("orb"), lax.axis_index("box")
    up, down = lax.rem(region + 1, regions), lax.rem(region + regions - 1, regions)
    mate = me + 1 - 2 * lax.rem(me, 2)
    peers = [lax.rem(me + 2 * d, blocks) for d in range(1, blocks // 2)]
    mates_peers = [lax.rem(mate + 2 * d, blocks) for d in range(1, blocks // 2)]
    others = [lax.rem(me + d, blocks) for d in range(1, blocks)]
    return me, region, up, down, mate, peers, mates_peers, others


def meet(me, region, up, down, others):
    barrier = pltpu.get_barrier_semaphore()
    devices = [(me, up), (me, down)] + [(o, region) for o in others]
    for device in devices:
        pl.semaphore_signal(barrier, inc=1, device_id=device, device_id_type=pl.DeviceIdType.MESH)
    pl.semaphore_wait(barrier, len(devices))


def remote(src, dst, send, recv, device):
    return pltpu.make_async_remote_copy(
        src_ref=src, dst_ref=dst, send_sem=send, recv_sem=recv, device_id=device,
        device_id_type=pl.DeviceIdType.MESH,
    )


def gather_kernel(dims, mine, meta, out, meta_out, send, recv, meta_send, meta_recv):
    box, own, blocks, regions = dims
    me, region, up, down, mate, peers, mates_peers, others = partners(blocks, regions)
    pieces = box // PIECE
    meet(me, region, up, down, others)
    sent = []

    def piece(o, s, k):
        return out.at[o, pl.ds(s * own, own), pl.ds(PIECE * k, PIECE)]

    def push(src, o, s, k, device):
        copy = remote(src, piece(o, s, k), send.at[len(sent)], recv.at[o, s, k], device)
        copy.start()
        sent.append(copy)

    def arrived(o, s, k):
        ref = piece(o, s, k)
        remote(ref, ref, send.at[0], recv.at[o, s, k], (mate, region)).wait_recv()

    for k in range(pieces):
        src = mine.at[:, pl.ds(PIECE * k, PIECE)]
        push(src, me, 0, k, (me, up))
        push(src, me, 2, k, (me, down))
    metas = []
    for n, o in enumerate(others):
        copy = remote(meta, meta_out.at[me], meta_send.at[n], meta_recv.at[me], (o, region))
        copy.start()
        metas.append(copy)
    for k in range(pieces):
        src = mine.at[:, pl.ds(PIECE * k, PIECE)]
        for peer in peers:
            push(src, me, 1, k, (peer, region))
        push(src, me, 1, k, (mate, region))
    out[me, pl.ds(own, own)] = mine[...]
    meta_out[me] = meta[...]
    for k in range(pieces):
        for s in (0, 2):
            arrived(me, s, k)
            for peer in peers:
                push(piece(me, s, k), me, s, k, (peer, region))
            push(piece(me, s, k), me, s, k, (mate, region))
        for peer in peers:
            arrived(peer, 1, k)
            push(piece(peer, 1, k), peer, 1, k, (mate, region))
    for k in range(pieces):
        for s in (0, 2):
            for peer in peers:
                arrived(peer, s, k)
                push(piece(peer, s, k), peer, s, k, (mate, region))
    for o in [mate] + mates_peers:
        for s in range(3):
            for k in range(pieces):
                arrived(o, s, k)
    for o in others:
        remote(meta, meta_out.at[o], meta_send.at[0], meta_recv.at[o], (mate, region)).wait_recv()
    for copy in sent + metas:
        copy.wait_send()


def reduce_kernel(
    dims, corners, cubes, totals, exchange, gram,
    held, mate_in, peer_out, peer_in, side_out, side_in, mid, columns,
    mate_send, mate_recv, peer_send, peer_recv, side_send, side_recv, col_send, col_recv,
):
    box, own, blocks, regions = dims
    region_size = own * blocks
    me, region, up, down, mate, peers, mates_peers, others = partners(blocks, regions)
    pieces = box // PIECE
    lane = lane_ids(box)
    steps = box // STEP
    zero8 = jnp.zeros((SPAN, LANES), F32)
    order = (0, 2, 1)
    meet(me, region, up, down, others)

    def part(ref, o, s, k):
        return ref.at[o, pl.ds(s * own, own), pl.ds(PIECE * k, PIECE)]

    def value(ref, o, s, k):
        return ref[o, pl.ds(s * own, own), pl.ds(PIECE * k, PIECE)].astype(F32)

    sent = []
    for t in mates_peers + [mate]:
        for s in order:
            for k in range(pieces):
                copy = remote(
                    part(totals, t, s, k), part(mate_in, t // 2, s, k),
                    mate_send.at[t // 2, s, k], mate_recv.at[t // 2, s, k], (mate, region),
                )
                copy.start()
                sent.append(copy)

    def from_mate(t, s, k):
        ref = part(mate_in, t // 2, s, k)
        remote(ref, ref, mate_send.at[0, 0, 0], mate_recv.at[t // 2, s, k], (mate, region)).wait_recv()

    for s in order:
        for k in range(pieces):
            for t in peers:
                from_mate(t, s, k)
                both = value(totals, t, s, k) + value(mate_in, t // 2, s, k)
                peer_out[t // 2, pl.ds(s * own, own), pl.ds(PIECE * k, PIECE)] = both.astype(BF16)
                copy = remote(
                    part(peer_out, t // 2, s, k), part(peer_in, me // 2, s, k),
                    peer_send.at[t // 2, s, k], peer_recv.at[me // 2, s, k], (t, region),
                )
                copy.start()
                sent.append(copy)

    def id_of(member):
        return ((member // own) * regions + region) * own + member % own

    def unpack(item, _):
        q, g = item // steps, item % steps
        halves = []
        for h in range(2):
            member = 2 * q + h
            halves.append(load_blocks(box, cubes, (member // own, own + member % own), g))
        for t, row in enumerate(unpack_pair(box, halves[0], halves[1], lane)):
            b = g * STEP + t
            held[q, b, :SPAN] = zero8
            held[q, b, SPAN : SPAN + box] = row
            held[q, b, SPAN + box :] = zero8
        return 0

    lax.fori_loop(0, region_size // 2 * steps, unpack, 0)

    for s in order:
        for k in range(pieces):
            from_mate(me, s, k)
            total = value(totals, me, s, k) + value(mate_in, me // 2, s, k)
            for t in peers:
                ref = part(peer_in, t // 2, s, k)
                remote(ref, ref, peer_send.at[0, 0, 0], peer_recv.at[t // 2, s, k], (t, region)).wait_recv()
                total = total + value(peer_in, t // 2, s, k)
            if s == 1:
                mid[:, pl.ds(PIECE * k, PIECE)] = total
                continue
            side = s // 2
            side_out[side, :, pl.ds(PIECE * k, PIECE)] = total.astype(BF16)
            copy = remote(
                side_out.at[side, :, pl.ds(PIECE * k, PIECE)], side_in.at[side, :, pl.ds(PIECE * k, PIECE)],
                side_send.at[side, k], side_recv.at[side, k], (me, down if s == 0 else up),
            )
            copy.start()
            sent.append(copy)
    for k in range(pieces):
        for side in range(2):
            ref = side_in.at[side, :, pl.ds(PIECE * k, PIECE)]
            remote(ref, ref, side_send.at[0, 0], side_recv.at[side, k], (me, up)).wait_recv()

    row8 = lax.broadcasted_iota(jnp.int32, (8, LANES), 0)
    lane8 = lane_ids(8)
    tile = jnp.zeros((8, LANES), F32)
    for col in range(own):
        mine = id_of(me * own + col)
        shifts = []
        for k in range(region_size):
            ck = id_of(k)
            shifts.append([corners[ck, d] - corners[mine, d] for d in range(3)])

        def step(g, sums):
            blocks_f = [
                a + b + c
                for a, b, c in zip(
                    load_blocks(box, mid, (col,), g),
                    load_blocks(box, side_in, (0, col), g),
                    load_blocks(box, side_in, (1, col), g),
                )
            ]
            start = pl.multiple_of(g * (box * STEP), LANES)
            for k, block in enumerate(blocks_f):
                exchange[col, :, pl.ds(start + LANES * k, LANES)] = block.astype(BF16)
            sums = list(sums)
            for t, (x, off) in enumerate(unpack_step(box, blocks_f, lane)):
                b = g * STEP + t
                x = pltpu.roll(x, (-off) % LANES, 1) if off else x
                x = jnp.where(lane < box, x, 0.0)
                for k in range(region_size):
                    e = shifts[k]
                    bj = b - e[1]
                    inside = jnp.logical_and(bj >= 0, bj < box).astype(F32)
                    at = jnp.clip(bj, 0, box - 1)
                    u = held[k // 2, at, pl.ds(SPAN - e[0], box)]
                    amount = lax.rem(e[2] + HALF * (k % 2) + LANES, LANES)
                    product = pltpu.roll(u, amount, 1) * x * inside
                    total = product[:8]
                    for r in range(8, box, 8):
                        total = total + product[r : r + 8]
                    sums[k] = sums[k] + total
            return tuple(sums)

        sums = lax.fori_loop(0, steps, step, tuple(jnp.zeros((8, LANES), F32) for _ in range(region_size)))
        for k in range(region_size):
            here = jnp.logical_and(row8 == k, lane8 == col)
            tile = jnp.where(here, jnp.sum(sums[k]) * (1.0 / box**3), tile)
    columns[me] = tile
    for n, o in enumerate(others):
        copy = remote(columns.at[me], columns.at[me], col_send.at[n], col_recv.at[me], (o, region))
        copy.start()
        sent.append(copy)
    for o in others:
        remote(columns.at[o], columns.at[o], col_send.at[0], col_recv.at[o], (mate, region)).wait_recv()
    whole = columns[0]
    for o in range(1, blocks):
        whole = whole + pltpu.roll(columns[o], o * own, 1)
    gram[0] = whole[:region_size, :region_size]
    for copy in sent:
        copy.wait_send()


def per_device(orbitals, corners, pairs, counts):
    own, box, plane = orbitals.shape
    blocks = lax.axis_size("orb")
    regions = lax.axis_size("box")
    region_size = own * blocks
    n_cubes = 3 * region_size
    dims = (box, own, blocks, regions)
    slots = pairs.shape[0]
    pieces = box // PIECE
    smem = pl.BlockSpec(memory_space=pltpu.SMEM)
    vmem = pl.BlockSpec(memory_space=pltpu.VMEM)
    dma = pltpu.SemaphoreType.DMA
    meta = jnp.stack([pairs[:, 0], pairs[:, 1], jnp.broadcast_to(counts[:1], (slots,))])
    meta = jnp.pad(meta, ((0, 5), (0, LANES - slots)))
    sends = pieces * (2 + 3 * (blocks - 1))
    gathered, metas = pl.pallas_call(
        functools.partial(gather_kernel, dims),
        out_shape=(
            jax.ShapeDtypeStruct((blocks, 3 * own, box, plane), BF16),
            jax.ShapeDtypeStruct((blocks, 8, LANES), jnp.int32),
        ),
        in_specs=[vmem, vmem],
        out_specs=(vmem, vmem),
        scratch_shapes=[
            dma((sends,)), dma((blocks, 3, pieces)), dma((blocks - 1,)), dma((blocks,)),
        ],
        compiler_params=pltpu.CompilerParams(
            collective_id=0, has_side_effects=True, vmem_limit_bytes=24 * 2**20
        ),
        name="gather_window",
    )(orbitals, meta)
    rows, lanes, green = tables(box)
    padded = (box, box + 2 * SPAN, LANES)
    taller = (box + 1, box + 2 * SPAN, LANES)
    totals = pl.pallas_call(
        functools.partial(pair_kernel, dims),
        out_shape=jax.ShapeDtypeStruct((n_cubes, box, plane), BF16),
        in_specs=[smem, smem, vmem, vmem, vmem, vmem],
        out_specs=vmem,
        scratch_shapes=[
            pltpu.VMEM((n_cubes // 2, *taller), F32),
            pltpu.VMEM((n_cubes // 2, *taller), F32),
            pltpu.VMEM((box * box, LANES), F32),
            pltpu.VMEM((box * box, LANES), F32),
            pltpu.VMEM((box, box, LANES), F32),
            pltpu.VMEM((box, box, LANES), F32),
        ],
        compiler_params=pltpu.CompilerParams(vmem_limit_bytes=60 * 2**20),
        name="pair_potentials",
    )(
        corners, metas, gathered.reshape(n_cubes, box, plane),
        jnp.asarray(rows), jnp.asarray(lanes), jnp.asarray(green),
    )
    chips = blocks // 2
    wide = (chips, 3 * own, box, plane)
    exchange, gram = pl.pallas_call(
        functools.partial(reduce_kernel, dims),
        out_shape=(
            jax.ShapeDtypeStruct((own, box, plane), BF16),
            jax.ShapeDtypeStruct((1, region_size, region_size), F32),
        ),
        in_specs=[smem, vmem, vmem],
        out_specs=(vmem, vmem),
        scratch_shapes=[
            pltpu.VMEM((region_size // 2, *padded), F32),
            pltpu.VMEM(wide, BF16),
            pltpu.VMEM(wide, BF16),
            pltpu.VMEM(wide, BF16),
            pltpu.VMEM((2, own, box, plane), BF16),
            pltpu.VMEM((2, own, box, plane), BF16),
            pltpu.VMEM((own, box, plane), F32),
            pltpu.VMEM((blocks, 8, LANES), F32),
            dma((chips, 3, pieces)), dma((chips, 3, pieces)),
            dma((chips, 3, pieces)), dma((chips, 3, pieces)),
            dma((2, pieces)), dma((2, pieces)),
            dma((blocks - 1,)), dma((blocks,)),
        ],
        compiler_params=pltpu.CompilerParams(
            collective_id=1, has_side_effects=True, vmem_limit_bytes=48 * 2**20
        ),
        name="reduce_and_gram",
    )(corners, gathered, totals.reshape(blocks, 3 * own, box, plane))
    return exchange, gram


def solution(mesh):
    placed = (P(("orb", "box"), None, None), P(), P(("orb", "box"), None), P(("orb", "box")))
    return jax.shard_map(
        per_device,
        mesh=mesh,
        in_specs=placed,
        out_specs=(P(("orb", "box"), None, None), P("box", None, None)),
        check_vma=False,
    )
```
